32 devices in a mesh: ctx: 4 (over y, x), tp: 8 (over z, core).
Axes of the slice: x: 2, y: 2, z: 4, core: 2. Of those that a mesh axis runs over, the one named last changes fastest.
Arguments:
- query_rows: bfloat16 [4096, 4096], P('ctx', 'tp'), may hold values from -6 to 6
- key_rows: bfloat16 [4096, 4096], P('ctx', 'tp'), may hold values from -0.5 to 0.5
- value_rows: bfloat16 [4096, 4096], P('ctx', 'tp'), may hold values from -500 to 500
- gate_logits: bfloat16 [4096, 4096], P('ctx', 'tp'), may hold values from -6 to 6
- norm_gain: float32 [4096], P('tp'), may hold values from 0.1 to 1.9
- log_decay: float32 [32, 4096], P('tp', 'ctx'), may hold values from -3 to 0
- offsets: int32 [6], replicated, may hold values from 0 to 4095, as said below
- cotangent: bfloat16 [4096, 4096], P('ctx', 'tp'), may hold values from -6 to 6
Outputs:
- attended: bfloat16 [4096, 4096], P('ctx', 'tp')
- grad_query: bfloat16 [4096, 4096], P('ctx', 'tp')
- grad_key: bfloat16 [4096, 4096], P('ctx', 'tp')
- grad_value: bfloat16 [4096, 4096], P('ctx', 'tp')
- grad_gate: bfloat16 [4096, 4096], P('ctx', 'tp')
The draws below stay inside these ranges and needn't reach their ends.
Inputs may be any that keep to these rules, and one draw needn't show every extreme that they name: offsets[0] is 0 and the entries rise strictly; each is the first token of a rollout; every entry after the first lies among the last 1024 tokens of the 4096.
All inputs are finite; a program needn't handle non-finite values.
Results may differ from the reference program's by a relative error of at most 0.0035.
Values sent between devices are 32-bit elements; how exact they have to be, the bound alone decides.
A program may use at most 128 MiB of HBM per device.

```python
import math
import jax
import jax.numpy as jnp
from jax import lax

D_HEAD = 128
HEAD_TOTAL = 32
TOK_DEV = 1024
TOKEN_TOTAL = 4096
BLOCK = 512
ROLLOUTS = 6


def draw_value_rows(key, part):
    key_base, key_row = jax.random.split(jax.random.fold_in(key, 11), 2)
    shape = (TOKEN_TOTAL, HEAD_TOTAL, D_HEAD)
    ladder = jnp.arange(HEAD_TOTAL, dtype=jnp.float32) / max(HEAD_TOTAL - 1, 1)
    head_scale = 3.0 ** ladder
    row_scale = jnp.exp(jax.random.uniform(key_row, (TOKEN_TOTAL, 1, 1), jnp.float32, 0.0, math.log(10.0)))
    base_value = jnp.clip(jax.random.normal(key_base, shape, jnp.float32), -6.0, 6.0)
    values = base_value * head_scale[None, :, None] * row_scale
    return values.reshape(TOKEN_TOTAL, HEAD_TOTAL * D_HEAD).astype(jnp.bfloat16)


def draw_log_decay(key, part):
    random_keys = jax.random.split(jax.random.fold_in(key, 23), 7)
    share = 0.5
    fast = jax.random.uniform(random_keys[0], (HEAD_TOTAL, 1), jnp.float32) < share
    fast_rate = 1.0 / jax.random.uniform(random_keys[1], (HEAD_TOTAL, 1), jnp.float32, 30.0, 50.0)
    slow_rate = jax.random.uniform(random_keys[2], (HEAD_TOTAL, 1), jnp.float32, 0.02, 0.12) / TOKEN_TOTAL
    base_value = jnp.where(fast, fast_rate, slow_rate)
    device_blocks = TOKEN_TOTAL // TOK_DEV
    log_two = math.log(2.0)
    device_share = jnp.exp(jax.random.uniform(random_keys[3], (HEAD_TOTAL, device_blocks, 1), jnp.float32, -log_two, log_two))
    device_share = jnp.broadcast_to(device_share, (HEAD_TOTAL, device_blocks, TOK_DEV)).reshape(HEAD_TOTAL, TOKEN_TOTAL)
    token_share = jnp.exp(jax.random.uniform(random_keys[4], (HEAD_TOTAL, TOKEN_TOTAL), jnp.float32, -log_two, log_two))
    surge_positions = jax.random.randint(random_keys[5], (HEAD_TOTAL, 2, 1), 0, TOKEN_TOTAL)
    surge_length = jax.random.uniform(random_keys[6], (HEAD_TOTAL, 2, 1), jnp.float32, math.log(0.5), math.log(0.8))
    chosen_positions = jnp.arange(TOKEN_TOTAL)[None, None, :]
    surge_groups = jnp.sum(jnp.where(chosen_positions == surge_positions, surge_length, 0.0), axis=1)
    return (-(base_value * device_share * token_share) + surge_groups).astype(jnp.float32)


def draw_offsets(key, part):
    lowest = TOKEN_TOTAL - TOK_DEV + 1
    picks = jax.random.permutation(jax.random.fold_in(key, 37), TOK_DEV - 1)[:ROLLOUTS - 1] + lowest
    return jnp.concatenate([jnp.zeros((1,), jnp.int32), jnp.sort(picks).astype(jnp.int32)])


def block_levels(own_key, extent, cuts, low, top_value):
    level, own = 1.0, jax.random.fold_in(own_key, 6)
    for axis_at, shards_of in cuts:
        heights = jnp.exp(jax.random.uniform(jax.random.fold_in(own, axis_at), (shards_of,), jnp.float32, low / len(cuts), top_value / len(cuts)))
        level = level * jnp.repeat(heights, extent[axis_at] // shards_of).reshape([-1 if axis == axis_at else 1 for axis in range(len(extent))])
    return level


def normal_values(stream_key, shape, scale, most, shards=(), held_as=jnp.bfloat16):
    values = jax.random.normal(stream_key, shape, jnp.float32) * scale
    if len(shards) > 0:
        values = block_levels(stream_key, shape, shards, -0.22, 0.18) * values
    return jnp.clip(values, min=-most, max=most).astype(held_as)


def setup_inputs(seed: int = 0) -> dict:
    key_of = jax.random.split(jax.random.key(seed), 9)
    return {
        "query_rows": normal_values(key_of[0], (TOKEN_TOTAL, HEAD_TOTAL * D_HEAD), 1.0, 6.0, ((0, 4), (1, 8))),
        "key_rows": normal_values(key_of[1], (TOKEN_TOTAL, HEAD_TOTAL * D_HEAD), D_HEAD ** -0.5, 0.5, ((0, 4), (1, 8))),
        "value_rows": draw_value_rows(jax.random.fold_in(key_of[8], 71), 0),
        "gate_logits": normal_values(key_of[3], (TOKEN_TOTAL, HEAD_TOTAL * D_HEAD), 1.5, 6.0, ((0, 4), (1, 8))),
        "norm_gain": jnp.clip(1.0 + 0.18 * jax.random.normal(key_of[4], (HEAD_TOTAL * D_HEAD,), jnp.float32), 0.1, 1.9),
        "log_decay": draw_log_decay(jax.random.fold_in(key_of[8], 71), 0),
        "offsets": draw_offsets(jax.random.fold_in(key_of[8], 71), 0),
        "cotangent": normal_values(key_of[7], (TOKEN_TOTAL, HEAD_TOTAL * D_HEAD), 1.0, 6.0, ((0, 4), (1, 8))),
    }


EPS_NORM = 1e-06
HIGHEST = lax.Precision.HIGHEST

def segment_ids(offsets, positions):
    hits = (offsets[None, :] <= positions[:, None]).astype(jnp.int32)
    return (lax.optimization_barrier(jnp.sum(hits, axis=1)) - 1).astype(jnp.int32)

def block_tables(decay_block, segment_block, segment_before):
    running = jnp.cumsum(decay_block)
    index_rows = jnp.arange(segment_block.shape[0])
    causal = (index_rows[None, :] <= index_rows[:, None]) & (segment_block[:, None] == segment_block[None, :])
    within = jnp.where(causal, jnp.exp(jnp.minimum(running[:, None] - running[None, :], 0.0)), 0.0)
    carry_weight = jnp.where(segment_block == segment_before, jnp.exp(running), 0.0)
    last_weight = jnp.where(segment_block == segment_block[-1], jnp.exp(jnp.minimum(running[-1] - running, 0.0)), 0.0)
    factor = jnp.where(segment_block[-1] == segment_before, jnp.exp(running[-1]), 0.0)
    return (within, carry_weight, last_weight, factor)

def head_forward(query_head, key_head, value_head, decay_head, segments, befores):

    def advance(carried, inputs):
        query_block, key_block, value_block, decay_block, segment_block, segment_before = inputs
        within, carry_weight, last_weight, factor = block_tables(decay_block, segment_block, segment_before)
        scores = jnp.dot(query_block, key_block.T, preferred_element_type=jnp.float32)
        weights = (scores * within).astype(jnp.bfloat16)
        query_f = query_block.astype(jnp.float32)
        key_f = key_block.astype(jnp.float32)
        value_f = value_block.astype(jnp.float32)
        output = jnp.dot(weights, value_block, preferred_element_type=jnp.float32) + carry_weight[:, None] * jnp.dot(query_f, carried, precision=HIGHEST)
        updated = factor * carried + jnp.dot((key_f * last_weight[:, None]).T, value_f, precision=HIGHEST)
        return (updated, (output, carried))
    initial = jnp.zeros((D_HEAD, D_HEAD), jnp.float32)
    _, (outputs, states) = lax.scan(advance, initial, (query_head, key_head, value_head, decay_head, segments, befores))
    return (outputs, states)

def head_backward(query_head, key_head, value_head, decay_head, segments, befores, states, grad_head):

    def retreat(coming, inputs):
        query_block, key_block, value_block, decay_block, segment_block, segment_before, state_block, grad_block = inputs
        within, carry_weight, last_weight, factor = block_tables(decay_block, segment_block, segment_before)
        scores = jnp.dot(query_block, key_block.T, preferred_element_type=jnp.float32)
        weights = (scores * within).astype(jnp.bfloat16)
        grad_low = grad_block.astype(jnp.bfloat16)
        query_f = query_block.astype(jnp.float32)
        key_f = key_block.astype(jnp.float32)
        value_f = value_block.astype(jnp.float32)
        back_scores = (jnp.dot(grad_low, value_block.T, preferred_element_type=jnp.float32) * within).astype(jnp.bfloat16)
        grad_q = jnp.dot(back_scores, key_block, preferred_element_type=jnp.float32) + carry_weight[:, None] * jnp.dot(grad_block, state_block.T, precision=HIGHEST)
        grad_k = jnp.dot(back_scores.T, query_block, preferred_element_type=jnp.float32) + last_weight[:, None] * jnp.dot(value_f, coming.T, precision=HIGHEST)
        grad_v = jnp.dot(weights.T, grad_low, preferred_element_type=jnp.float32) + last_weight[:, None] * jnp.dot(key_f, coming, precision=HIGHEST)
        earlier = factor * coming + jnp.dot((query_f * carry_weight[:, None]).T, grad_block, precision=HIGHEST)
        return (earlier, (grad_q, grad_k, grad_v))
    initial = jnp.zeros((D_HEAD, D_HEAD), jnp.float32)
    _, grads = lax.scan(retreat, initial, (query_head, key_head, value_head, decay_head, segments, befores, states, grad_head), reverse=True)
    return grads

def reference(query_rows, key_rows, value_rows, gate_logits, norm_gain, log_decay, offsets, cotangent):
    head_count = log_decay.shape[0]
    token_count = query_rows.shape[0]
    block_count = token_count // BLOCK
    feature_total = head_count * D_HEAD
    positions = jnp.arange(token_count, dtype=jnp.int32)
    segments = segment_ids(offsets, positions).reshape(block_count, BLOCK)
    starts = positions.reshape(block_count, BLOCK)[:, 0]
    befores = segment_ids(offsets, (starts - 1).astype(jnp.int32))

    def to_heads(array):
        return array.reshape(block_count, BLOCK, head_count, D_HEAD).transpose(2, 0, 1, 3)

    def from_heads(array):
        return array.transpose(1, 2, 0, 3).reshape(token_count, feature_total).astype(jnp.bfloat16)
    queries = to_heads(query_rows)
    key_heads = to_heads(key_rows)
    value_heads = to_heads(value_rows)
    decays = log_decay.reshape(head_count, block_count, BLOCK)

    def forward_one(inputs):
        return head_forward(inputs[0], inputs[1], inputs[2], inputs[3], segments, befores)
    attention, states = lax.map(forward_one, (queries, key_heads, value_heads, decays))
    squares = lax.optimization_barrier(jnp.sum(attention * attention, axis=(0, 3)))
    rms = jnp.sqrt(squares / feature_total + EPS_NORM)[None, :, :, None]
    normed = attention / rms
    gain_heads = norm_gain.reshape(head_count, 1, 1, D_HEAD)
    gate_sig = jax.nn.sigmoid(to_heads(gate_logits).astype(jnp.float32))
    attended = normed * gain_heads * gate_sig
    upstream = to_heads(cotangent).astype(jnp.float32)
    grad_gate = upstream * normed * gain_heads * gate_sig * (1.0 - gate_sig)
    grad_normed = upstream * gain_heads * gate_sig
    inner = lax.optimization_barrier(jnp.sum(grad_normed * normed, axis=(0, 3)))[None, :, :, None]
    grad_attn = (grad_normed - normed * (inner / feature_total)) / rms

    def backward_one(inputs):
        return head_backward(inputs[0], inputs[1], inputs[2], inputs[3], segments, befores, inputs[4], inputs[5])
    grad_query, grad_key, grad_value = lax.map(backward_one, (queries, key_heads, value_heads, decays, states, grad_attn))
    return (from_heads(attended), from_heads(grad_query), from_heads(grad_key), from_heads(grad_value), from_heads(grad_gate))
```

```python
import functools

import jax
import jax.numpy as jnp
from jax import lax
from jax.experimental import pallas as pl
from jax.experimental.pallas import tpu as pltpu
from jax.sharding import PartitionSpec as P

D_HEAD = 128
BLOCK = 512
HALF = 256
LANES = 128
EPS_NORM = 1e-06
MASKED = -1000.0
MESH = pl.DeviceIdType.MESH
F32 = jnp.float32
BF16 = jnp.bfloat16


def split(value):
    high = value.astype(BF16)
    return high, (value - high.astype(F32)).astype(BF16)


def dot(left, right, dims):
    return lax.dot_general(left, right, (dims, ((), ())), preferred_element_type=F32)


def mm(left, right):
    return dot(left, right, ((1,), (0,)))


def mm_rt(left, right):
    return dot(left, right, ((1,), (1,)))


def mm_lt(left, right):
    return dot(left, right, ((0,), (0,)))


def times_state(rows, state):
    return mm(jnp.concatenate([rows, rows], axis=1), jnp.concatenate(split(state), axis=0))


def times_state_t(rows, state):
    return mm_rt(jnp.concatenate([rows, rows], axis=1), jnp.concatenate(split(state), axis=1))


def outer_state(rows, weighted):
    both = mm_lt(rows, jnp.concatenate(split(weighted), axis=1))
    return both[:, :D_HEAD] + both[:, D_HEAD:]


def kernel(
    ctx_count, tp_count, heads, blocks,
    offs, q_ref, k_ref, v_ref, gate_ref, gain_ref, decay_ref, cot_ref,
    att_ref, dq_ref, dk_ref, dv_ref, dg_ref,
    run_row, run_col, carry, last, factor, bias, within, weights,
    attn, sig, gattn, key_acc, value_acc, states, local_state, back_state,
    total, prefix, send_state, recv_state, sums, recv_sums, scale_col,
    send_sem, recv_sem, sum_send_sem, sum_recv_sem,
):
    ctx = lax.axis_index("ctx")
    tp = lax.axis_index("tp")
    steps = (ctx_count - 1).bit_length()
    features = tp_count * heads * D_HEAD
    offset_count = offs.shape[0]

    def partner(step):
        size = 1 << step
        return ctx + size * (1 - 2 * ((ctx // size) % 2))

    def peer(hop):
        return lax.rem(tp + hop, tp_count)

    barrier = pltpu.get_barrier_semaphore()
    for step in range(steps):
        pl.semaphore_signal(barrier, inc=1, device_id=(partner(step), tp), device_id_type=MESH)
    for hop in range(1, tp_count):
        pl.semaphore_signal(barrier, inc=1, device_id=(ctx, peer(hop)), device_id_type=MESH)

    first = ctx * (blocks * BLOCK)

    def segment(positions):
        count = (offs[0] <= positions).astype(jnp.int32)
        for entry in range(1, offset_count):
            count = count + (offs[entry] <= positions).astype(jnp.int32)
        return count

    decays = jnp.concatenate(
        [decay_ref[:, b * BLOCK:(b + 1) * BLOCK] for b in range(blocks)], axis=0
    )
    rest = decays
    pieces = []
    for _ in range(3):
        piece = rest.astype(BF16)
        pieces.append(piece)
        rest = rest - piece.astype(F32)
    lower = lax.broadcasted_iota(jnp.int32, (BLOCK, BLOCK), 0)
    upper = lax.broadcasted_iota(jnp.int32, (BLOCK, BLOCK), 1)
    summing = jnp.where(lower <= upper, 1.0, 0.0).astype(BF16)
    running = mm(pieces[2], summing) + mm(pieces[1], summing) + mm(pieces[0], summing)
    run_row[...] = running
    lane = lax.broadcasted_iota(jnp.int32, (1, BLOCK), 1)
    sub = lax.broadcasted_iota(jnp.int32, (BLOCK, 1), 0)
    carry_rows, last_rows = [], []
    for b in range(blocks):
        start = first + b * BLOCK
        rows = running[b * heads:(b + 1) * heads]
        seg_row = segment(start + lane)
        seg_col = segment(start + sub)
        before = segment(start - 1)
        final = segment(start + BLOCK - 1)
        bias[b] = jnp.where((seg_col == seg_row) & (lower >= upper), 0.0, MASKED)
        carry_rows.append(jnp.where(seg_row == before, jnp.exp(rows), 0.0))
        end = rows[:, BLOCK - 1:]
        last_rows.append(jnp.where(seg_row == final, jnp.exp(jnp.minimum(end - rows, 0.0)), 0.0))
        whole = jnp.where(before == final, jnp.exp(end), 0.0)
        factor[b * heads:(b + 1) * heads, :] = jnp.broadcast_to(whole, (heads, LANES))
    count = heads * blocks
    stacked = jnp.concatenate(
        [running] + carry_rows + last_rows + [jnp.zeros((LANES - 3 * count, BLOCK), F32)], axis=0
    )
    columns = stacked.T
    for r in range(count):
        run_col[r] = jnp.broadcast_to(columns[:, r:r + 1], (BLOCK, LANES))
        carry[r] = jnp.broadcast_to(columns[:, count + r:count + r + 1], (BLOCK, LANES))
        last[r] = jnp.broadcast_to(columns[:, 2 * count + r:2 * count + r + 1], (BLOCK, LANES))

    def head_cols(h):
        return pl.ds(pl.multiple_of(h * D_HEAD, D_HEAD), D_HEAD)

    def block_rows(b):
        return pl.ds(b * BLOCK, BLOCK)

    def factor_of(b, h):
        return factor[pl.ds(b * heads + h, 1), :]

    def summarize(h, _):
        cols = head_cols(h)
        acc = None
        prod = None
        for b in range(blocks):
            r = b * heads + h
            weighted = v_ref[block_rows(b), cols].astype(F32) * last[r]
            state = outer_state(k_ref[block_rows(b), cols], weighted)
            local_state[r] = state
            fac = factor_of(b, h)
            acc = state if acc is None else fac * acc + state
            prod = fac if prod is None else prod * fac
        total[h, :D_HEAD, :] = acc
        total[h, D_HEAD:, :] = jnp.broadcast_to(prod, (8, LANES))
        return 0

    lax.fori_loop(0, heads, summarize, 0)
    pl.semaphore_wait(barrier, steps + tp_count - 1)

    def exchange(way, step, h):
        return pltpu.make_async_remote_copy(
            src_ref=send_state.at[way, step, h],
            dst_ref=recv_state.at[way, step, h],
            send_sem=send_sem.at[way, step, h],
            recv_sem=recv_sem.at[way, step, h],
            device_id=(partner(step), tp),
            device_id_type=MESH,
        )

    def begin(way):
        for h in range(heads):
            prefix[h, :D_HEAD, :] = jnp.zeros((D_HEAD, LANES), F32)
            prefix[h, D_HEAD:, :] = jnp.ones((8, LANES), F32)
            send_state[way, 0, h] = total[h]
            exchange(way, 0, h).start()

    def advance(way, step, h):
        exchange(way, step, h).wait()
        size = 1 << step
        bit = (ctx // size) % 2
        after = bit == 1 if way == 0 else bit == 0
        other = recv_state[way, step, h, :D_HEAD, :]
        other_factor = recv_state[way, step, h, D_HEAD:, :][:1]
        mine = total[h, :D_HEAD, :]
        my_factor = total[h, D_HEAD:, :][:1]
        so_far = prefix[h, :D_HEAD, :]
        so_far_factor = prefix[h, D_HEAD:, :][:1]
        prefix[h, :D_HEAD, :] = jnp.where(after, so_far_factor * other + so_far, so_far)
        prefix[h, D_HEAD:, :] = jnp.broadcast_to(
            jnp.where(after, so_far_factor * other_factor, so_far_factor), (8, LANES)
        )
        if step + 1 < steps:
            joined = jnp.where(after, my_factor * other + mine, other_factor * mine + other)
            total[h, :D_HEAD, :] = joined
            total[h, D_HEAD:, :] = jnp.broadcast_to(my_factor * other_factor, (8, LANES))
            send_state[way, step + 1, h] = total[h]
            exchange(way, step + 1, h).start()

    begin(0)

    def attend(h, _):
        cols = head_cols(h)
        for b in range(blocks):
            r = b * heads + h
            rows = block_rows(b)
            query, key, value = q_ref[rows, cols], k_ref[rows, cols], v_ref[rows, cols]
            for top, bottom in ((0, HALF), (HALF, BLOCK)):
                col = run_col[r, top:bottom, :]
                col = jnp.concatenate([col] * (bottom // LANES), axis=1)
                row = run_row[pl.ds(r, 1), :][:, :bottom]
                decay = jnp.exp(jnp.minimum(col - row, bias[b, top:bottom, :bottom]))
                within[r, top:bottom, :bottom] = decay
                scores = mm_rt(query[top:bottom], key[:bottom])
                weight = (scores * decay).astype(BF16)
                weights[r, top:bottom, :bottom] = weight
                attn[r, top:bottom, :] = mm(weight, value[:bottom])
            sig[r] = jax.nn.sigmoid(gate_ref[rows, cols].astype(F32))
        return 0

    lax.fori_loop(0, heads, attend, 0)
    for step in range(steps):
        for h in range(heads):
            advance(0, step, h)

    def sum_copy(b, hop):
        return pltpu.make_async_remote_copy(
            src_ref=sums.at[b],
            dst_ref=recv_sums.at[b, hop - 1],
            send_sem=sum_send_sem.at[b, hop - 1],
            recv_sem=sum_recv_sem.at[b, hop - 1],
            device_id=(ctx, peer(hop)),
            device_id_type=MESH,
        )

    def upstream(rows, cols, r):
        return cot_ref[rows, cols].astype(F32) * (gain_ref[:, cols] * sig[r])

    ones = jnp.ones((8, 2 * LANES), BF16)
    chunks = BLOCK // LANES
    for b in range(blocks):
        rows = block_rows(b)

        def carry_in(h, acc, b=b, rows=rows):
            cols = head_cols(h)
            r = b * heads + h
            state = prefix[h, :D_HEAD, :]
            states[r] = state
            value = attn[r] + carry[r] * times_state(q_ref[rows, cols], state)
            attn[r] = value
            prefix[h, :D_HEAD, :] = factor_of(b, h) * state + local_state[r]
            return acc[0] + value * value, acc[1] + upstream(rows, cols, r) * value

        zero = jnp.zeros((BLOCK, LANES), F32)
        squares, inners = lax.fori_loop(0, heads, carry_in, (zero, zero))
        for at, part in ((0, squares), (chunks, inners)):
            line = mm_rt(ones, jnp.concatenate(split(part), axis=1))
            for c in range(chunks):
                sums[b, at + c:at + c + 1, :] = line[:1, c * LANES:(c + 1) * LANES]
        for hop in range(1, tp_count):
            sum_copy(b, hop).start()

    for b in range(blocks):
        rows = block_rows(b)
        added = sums[b]
        for hop in range(1, tp_count):
            sum_copy(b, hop).wait()
            added = added + recv_sums[b, hop - 1]
        inverse = 1.0 / jnp.sqrt(added[:chunks] / features + EPS_NORM)
        mean_inner = added[chunks:] * inverse / features
        turned = jnp.concatenate(
            [inverse, mean_inner, jnp.zeros((LANES - 2 * chunks, LANES), F32)], axis=0
        ).T
        for c in range(chunks):
            here = pl.ds(c * LANES, LANES)
            scale_col[b, 0, here, :] = jnp.broadcast_to(turned[:, c:c + 1], (LANES, LANES))
            scale_col[b, 1, here, :] = jnp.broadcast_to(
                turned[:, chunks + c:chunks + c + 1], (LANES, LANES)
            )

        def grad_in(h, _, b=b, rows=rows):
            cols = head_cols(h)
            r = b * heads + h
            inv = scale_col[b, 0]
            grad = (upstream(rows, cols, r) - attn[r] * inv * scale_col[b, 1]) * inv
            gattn[r] = grad
            back_state[r] = outer_state(q_ref[rows, cols], grad * carry[r])
            return 0

        lax.fori_loop(0, heads, grad_in, 0)

    def summarize_back(h, _):
        acc = None
        prod = None
        for b in range(blocks - 1, -1, -1):
            r = b * heads + h
            fac = factor_of(b, h)
            acc = back_state[r] if acc is None else fac * acc + back_state[r]
            prod = fac if prod is None else prod * fac
        total[h, :D_HEAD, :] = acc
        total[h, D_HEAD:, :] = jnp.broadcast_to(prod, (8, LANES))
        return 0

    lax.fori_loop(0, heads, summarize_back, 0)
    begin(1)

    def retreat(h, _):
        cols = head_cols(h)
        for b in range(blocks):
            r = b * heads + h
            rows = block_rows(b)
            query, key, value = q_ref[rows, cols], k_ref[rows, cols], v_ref[rows, cols]
            normed = attn[r] * scale_col[b, 0]
            gate = sig[r]
            gated = normed * (gain_ref[:, cols] * gate)
            att_ref[rows, cols] = gated.astype(BF16)
            dg_ref[rows, cols] = (cot_ref[rows, cols].astype(F32) * gated * (1.0 - gate)).astype(BF16)
            high, low = split(gattn[r])
            state_high, state_low = split(states[r])
            crossed = mm_rt(
                jnp.concatenate([high, low], axis=1),
                jnp.concatenate([state_high, state_high], axis=1),
            ) + mm_rt(high, state_low)
            crossed = carry[r] * crossed
            back = []
            for top, bottom in ((0, HALF), (HALF, BLOCK)):
                scores = mm_rt(high[top:bottom], value[:bottom])
                piece = (scores * within[r, top:bottom, :bottom]).astype(BF16)
                back.append(piece)
                dq_ref[pl.ds(b * BLOCK + top, HALF), cols] = (
                    mm(piece, key[:bottom]) + crossed[top:bottom]
                ).astype(BF16)
            key_acc[r] = mm_lt(back[1], query[HALF:])
            key_acc[r, :HALF, :] += mm_lt(back[0], query[:HALF])
            value_acc[r] = mm_lt(weights[r, HALF:, :], high[HALF:])
            value_acc[r, :HALF, :] += mm_lt(weights[r, :HALF, :HALF], high[:HALF])
        return 0

    lax.fori_loop(0, heads, retreat, 0)
    for step in range(steps):
        for h in range(heads):
            advance(1, step, h)

    def finish(h, _):
        cols = head_cols(h)
        coming = prefix[h, :D_HEAD, :]
        for b in range(blocks - 1, -1, -1):
            r = b * heads + h
            rows = block_rows(b)
            dk_ref[rows, cols] = (
                key_acc[r] + last[r] * times_state_t(v_ref[rows, cols], coming)
            ).astype(BF16)
            dv_ref[rows, cols] = (
                value_acc[r] + last[r] * times_state(k_ref[rows, cols], coming)
            ).astype(BF16)
            if b > 0:
                coming = factor_of(b, h) * coming + back_state[r]
        return 0

    lax.fori_loop(0, heads, finish, 0)


def local(ctx_count, tp_count, query_rows, key_rows, value_rows, gate_logits, norm_gain, log_decay,
          offsets, cotangent):
    heads = log_decay.shape[0]
    tokens, width = query_rows.shape
    blocks = tokens // BLOCK
    count = heads * blocks
    steps = (ctx_count - 1).bit_length()
    out = jax.ShapeDtypeStruct((tokens, width), BF16)
    vmem = pl.BlockSpec(memory_space=pltpu.VMEM)
    tile = (count, BLOCK, LANES)
    state = (count, D_HEAD, D_HEAD)
    message = (heads, D_HEAD + 8, LANES)
    return pl.pallas_call(
        functools.partial(kernel, ctx_count, tp_count, heads, blocks),
        out_shape=(out,) * 5,
        in_specs=[pl.BlockSpec(memory_space=pltpu.SMEM)] + [vmem] * 7,
        out_specs=(vmem,) * 5,
        scratch_shapes=[
            pltpu.VMEM((count, BLOCK), F32),
            pltpu.VMEM(tile, F32),
            pltpu.VMEM(tile, F32),
            pltpu.VMEM(tile, F32),
            pltpu.VMEM((count, LANES), F32),
            pltpu.VMEM((blocks, BLOCK, BLOCK), F32),
            pltpu.VMEM((count, BLOCK, BLOCK), F32),
            pltpu.VMEM((count, BLOCK, BLOCK), BF16),
            pltpu.VMEM(tile, F32),
            pltpu.VMEM(tile, F32),
            pltpu.VMEM(tile, F32),
            pltpu.VMEM(tile, F32),
            pltpu.VMEM(tile, F32),
            pltpu.VMEM(state, F32),
            pltpu.VMEM(state, F32),
            pltpu.VMEM(state, F32),
            pltpu.VMEM(message, F32),
            pltpu.VMEM(message, F32),
            pltpu.VMEM((2, steps) + message, F32),
            pltpu.VMEM((2, steps) + message, F32),
            pltpu.VMEM((blocks, 8, LANES), F32),
            pltpu.VMEM((blocks, tp_count - 1, 8, LANES), F32),
            pltpu.VMEM((blocks, 2, BLOCK, LANES), F32),
            pltpu.SemaphoreType.DMA((2, steps, heads)),
            pltpu.SemaphoreType.DMA((2, steps, heads)),
            pltpu.SemaphoreType.DMA((blocks, tp_count - 1)),
            pltpu.SemaphoreType.DMA((blocks, tp_count - 1)),
        ],
        compiler_params=pltpu.CompilerParams(
            collective_id=0, has_side_effects=True, vmem_limit_bytes=56 * 1024 * 1024
        ),
    )(
        offsets, query_rows, key_rows, value_rows, gate_logits,
        norm_gain.reshape(1, width), log_decay, cotangent,
    )


def solution(mesh):
    rows = P("ctx", "tp")
    return jax.shard_map(
        functools.partial(local, mesh.shape["ctx"], mesh.shape["tp"]),
        mesh=mesh,
        in_specs=(rows, rows, rows, rows, P("tp"), P("tp", "ctx"), P(), rows),
        out_specs=(rows,) * 5,
        check_vma=False,
    )
```

```python
import functools

import jax
import jax.numpy as jnp
from jax import lax
from jax.experimental import pallas as pl
from jax.experimental.pallas import tpu as pltpu
from jax.sharding import PartitionSpec as P

D_HEAD = 128
BLOCK = 512
HALF = 256
LANES = 128
EPS_NORM = 1e-06
MASKED = -1000.0
MESH = pl.DeviceIdType.MESH
F32 = jnp.float32
BF16 = jnp.bfloat16


def split(value):
    high = value.astype(BF16)
    return high, (value - high.astype(F32)).astype(BF16)


def dot(left, right, dims):
    return lax.dot_general(left, right, (dims, ((), ())), preferred_element_type=F32)


def mm(left, right):
    return dot(left, right, ((1,), (0,)))


def mm_rt(left, right):
    return dot(left, right, ((1,), (1,)))


def mm_lt(left, right):
    return dot(left, right, ((0,), (0,)))


def times_state(rows, state):
    return mm(jnp.concatenate([rows, rows], axis=1), jnp.concatenate(split(state), axis=0))


def times_state_t(rows, state):
    return mm_rt(jnp.concatenate([rows, rows], axis=1), jnp.concatenate(split(state), axis=1))


def outer_state(rows, weighted):
    both = mm_lt(rows, jnp.concatenate(split(weighted), axis=1))
    return both[:, :D_HEAD] + both[:, D_HEAD:]


def kernel(
    ctx_count, tp_count, heads, blocks,
    offs, q_hbm, k_hbm, v_hbm, gate_hbm, gain_ref, decay_ref, cot_hbm,
    att_ref, dq_ref, dg_ref, key_acc, value_acc, last, factor, back_state, prefix,
    run_row, run_col, carry, bias, within, weights,
    attn, sig, gattn, states, local_state,
    total, send_state, recv_state, sums, recv_sums, scale_col,
    q_ref, k_ref, v_ref, gate_ref, cot_ref,
    send_sem, recv_sem, sum_send_sem, sum_recv_sem, load_sem,
):
    loads = [
        pltpu.make_async_copy(src, dst, load_sem.at[i])
        for i, (src, dst) in enumerate((
            (k_hbm, k_ref), (v_hbm, v_ref), (q_hbm, q_ref), (gate_hbm, gate_ref), (cot_hbm, cot_ref),
        ))
    ]
    for load in loads:
        load.start()
    ctx = lax.axis_index("ctx")
    tp = lax.axis_index("tp")
    steps = (ctx_count - 1).bit_length()
    features = tp_count * heads * D_HEAD
    offset_count = offs.shape[0]

    def partner(step):
        size = 1 << step
        return ctx + size * (1 - 2 * ((ctx // size) % 2))

    def peer(hop):
        return lax.rem(tp + hop, tp_count)

    barrier = pltpu.get_barrier_semaphore()
    for step in range(steps):
        pl.semaphore_signal(barrier, inc=1, device_id=(partner(step), tp), device_id_type=MESH)
    for hop in range(1, tp_count):
        pl.semaphore_signal(barrier, inc=1, device_id=(ctx, peer(hop)), device_id_type=MESH)

    first = ctx * (blocks * BLOCK)

    def segment(positions):
        count = (offs[0] <= positions).astype(jnp.int32)
        for entry in range(1, offset_count):
            count = count + (offs[entry] <= positions).astype(jnp.int32)
        return count

    decays = jnp.concatenate(
        [decay_ref[:, b * BLOCK:(b + 1) * BLOCK] for b in range(blocks)], axis=0
    )
    rest = decays
    pieces = []
    for _ in range(3):
        piece = rest.astype(BF16)
        pieces.append(piece)
        rest = rest - piece.astype(F32)
    lower = lax.broadcasted_iota(jnp.int32, (BLOCK, BLOCK), 0)
    upper = lax.broadcasted_iota(jnp.int32, (BLOCK, BLOCK), 1)
    summing = jnp.where(lower <= upper, 1.0, 0.0).astype(BF16)
    running = mm(pieces[2], summing) + mm(pieces[1], summing) + mm(pieces[0], summing)
    run_row[...] = running
    lane = lax.broadcasted_iota(jnp.int32, (1, BLOCK), 1)
    sub = lax.broadcasted_iota(jnp.int32, (BLOCK, 1), 0)
    carry_rows, last_rows = [], []
    for b in range(blocks):
        start = first + b * BLOCK
        rows = running[b * heads:(b + 1) * heads]
        seg_row = segment(start + lane)
        seg_col = segment(start + sub)
        before = segment(start - 1)
        final = segment(start + BLOCK - 1)
        bias[b] = jnp.where((seg_col == seg_row) & (lower >= upper), 0.0, MASKED)
        carry_rows.append(jnp.where(seg_row == before, jnp.exp(rows), 0.0))
        end = rows[:, BLOCK - 1:]
        last_rows.append(jnp.where(seg_row == final, jnp.exp(jnp.minimum(end - rows, 0.0)), 0.0))
        whole = jnp.where(before == final, jnp.exp(end), 0.0)
        factor[b * heads:(b + 1) * heads, :] = jnp.broadcast_to(whole, (heads, LANES))
    count = heads * blocks
    stacked = jnp.concatenate(
        [running] + carry_rows + last_rows + [jnp.zeros((LANES - 3 * count, BLOCK), F32)], axis=0
    )
    columns = stacked.T
    for r in range(count):
        run_col[r] = jnp.broadcast_to(columns[:, r:r + 1], (BLOCK, LANES))
        carry[r] = jnp.broadcast_to(columns[:, count + r:count + r + 1], (BLOCK, LANES))
        last[r] = jnp.broadcast_to(columns[:, 2 * count + r:2 * count + r + 1], (BLOCK, LANES))

    def head_cols(h):
        return pl.ds(pl.multiple_of(h * D_HEAD, D_HEAD), D_HEAD)

    def block_rows(b):
        return pl.ds(b * BLOCK, BLOCK)

    def factor_of(b, h):
        return factor[pl.ds(b * heads + h, 1), :]

    def exchange(way, step, h):
        return pltpu.make_async_remote_copy(
            src_ref=send_state.at[way, step, h],
            dst_ref=recv_state.at[way, step, h],
            send_sem=send_sem.at[way, step, h],
            recv_sem=recv_sem.at[way, step, h],
            device_id=(partner(step), tp),
            device_id_type=MESH,
        )

    def begin(way, h, state, state_factor):
        prefix[h, :D_HEAD, :] = jnp.zeros((D_HEAD, LANES), F32)
        prefix[h, D_HEAD:, :] = jnp.ones((8, LANES), F32)
        spread = jnp.broadcast_to(state_factor, (8, LANES))
        total[h, :D_HEAD, :] = state
        total[h, D_HEAD:, :] = spread
        send_state[way, 0, h, :D_HEAD, :] = state
        send_state[way, 0, h, D_HEAD:, :] = spread
        exchange(way, 0, h).start()

    def advance(way, step, h):
        exchange(way, step, h).wait()
        size = 1 << step
        bit = (ctx // size) % 2
        after = bit == 1 if way == 0 else bit == 0
        other = recv_state[way, step, h, :D_HEAD, :]
        other_factor = recv_state[way, step, h, D_HEAD:, :][:1]
        mine = total[h, :D_HEAD, :]
        my_factor = total[h, D_HEAD:, :][:1]
        if step + 1 < steps:
            joined = jnp.where(after, my_factor * other + mine, other_factor * mine + other)
            spread = jnp.broadcast_to(my_factor * other_factor, (8, LANES))
            send_state[way, step + 1, h, :D_HEAD, :] = joined
            send_state[way, step + 1, h, D_HEAD:, :] = spread
            exchange(way, step + 1, h).start()
            total[h, :D_HEAD, :] = joined
            total[h, D_HEAD:, :] = spread
        so_far = prefix[h, :D_HEAD, :]
        so_far_factor = prefix[h, D_HEAD:, :][:1]
        prefix[h, :D_HEAD, :] = jnp.where(after, so_far_factor * other + so_far, so_far)
        prefix[h, D_HEAD:, :] = jnp.broadcast_to(
            jnp.where(after, so_far_factor * other_factor, so_far_factor), (8, LANES)
        )

    def advance_rest(way):
        for step in range(1, steps - 1):
            for h in range(heads):
                advance(way, step, h)

    pl.semaphore_wait(barrier, steps + tp_count - 1)
    loads[0].wait()
    loads[1].wait()

    def summarize(h, _):
        cols = head_cols(h)
        acc = None
        prod = None
        for b in range(blocks):
            r = b * heads + h
            weighted = v_ref[block_rows(b), cols].astype(F32) * last[r]
            state = outer_state(k_ref[block_rows(b), cols], weighted)
            local_state[r] = state
            fac = factor_of(b, h)
            acc = state if acc is None else fac * acc + state
            prod = fac if prod is None else prod * fac
        begin(0, h, acc, prod)
        return 0

    lax.fori_loop(0, heads, summarize, 0)

    loads[2].wait()
    loads[3].wait()
    def attend(h, _):
        cols = head_cols(h)
        for b in range(blocks):
            r = b * heads + h
            rows = block_rows(b)
            query, key, value = q_ref[rows, cols], k_ref[rows, cols], v_ref[rows, cols]
            for top, bottom in ((0, HALF), (HALF, BLOCK)):
                col = run_col[r, top:bottom, :]
                col = jnp.concatenate([col] * (bottom // LANES), axis=1)
                row = run_row[pl.ds(r, 1), :][:, :bottom]
                decay = jnp.exp(jnp.minimum(col - row, bias[b, top:bottom, :bottom]))
                within[r, top:bottom, :bottom] = decay
                scores = mm_rt(query[top:bottom], key[:bottom])
                weight = (scores * decay).astype(BF16)
                weights[r, top:bottom, :bottom] = weight
                attn[r, top:bottom, :] = mm(weight, value[:bottom])
            sig[r] = jax.nn.sigmoid(gate_ref[rows, cols].astype(F32))
        if steps > 1:
            advance(0, 0, h)
        return 0

    lax.fori_loop(0, heads, attend, 0)
    advance_rest(0)
    loads[4].wait()

    def sum_copy(b, hop):
        return pltpu.make_async_remote_copy(
            src_ref=sums.at[b],
            dst_ref=recv_sums.at[b, hop - 1],
            send_sem=sum_send_sem.at[b, hop - 1],
            recv_sem=sum_recv_sem.at[b, hop - 1],
            device_id=(ctx, peer(hop)),
            device_id_type=MESH,
        )

    def upstream(rows, cols, r):
        return cot_ref[rows, cols].astype(F32) * (gain_ref[:, cols] * sig[r])

    ones = jnp.ones((8, 2 * LANES), BF16)
    chunks = BLOCK // LANES
    for b in range(blocks):
        rows = block_rows(b)

        def carry_in(h, acc, b=b, rows=rows):
            cols = head_cols(h)
            r = b * heads + h
            if b == 0 and steps > 0:
                advance(0, steps - 1, h)
            state = prefix[h, :D_HEAD, :]
            states[r] = state
            value = attn[r] + carry[r] * times_state(q_ref[rows, cols], state)
            attn[r] = value
            prefix[h, :D_HEAD, :] = factor_of(b, h) * state + local_state[r]
            return acc[0] + value * value, acc[1] + upstream(rows, cols, r) * value

        zero = jnp.zeros((BLOCK, LANES), F32)
        squares, inners = lax.fori_loop(0, heads, carry_in, (zero, zero))
        for at, part in ((0, squares), (chunks, inners)):
            line = mm_rt(ones, jnp.concatenate(split(part), axis=1))
            for c in range(chunks):
                sums[b, at + c:at + c + 1, :] = line[:1, c * LANES:(c + 1) * LANES]
        for hop in range(1, tp_count):
            sum_copy(b, hop).start()

    for b in range(blocks):
        rows = block_rows(b)
        added = sums[b]
        for hop in range(1, tp_count):
            sum_copy(b, hop).wait()
            added = added + recv_sums[b, hop - 1]
        inverse = 1.0 / jnp.sqrt(added[:chunks] / features + EPS_NORM)
        mean_inner = added[chunks:] * inverse / features
        turned = jnp.concatenate(
            [inverse, mean_inner, jnp.zeros((LANES - 2 * chunks, LANES), F32)], axis=0
        ).T
        for c in range(chunks):
            here = pl.ds(c * LANES, LANES)
            scale_col[b, 0, here, :] = jnp.broadcast_to(turned[:, c:c + 1], (LANES, LANES))
            scale_col[b, 1, here, :] = jnp.broadcast_to(
                turned[:, chunks + c:chunks + c + 1], (LANES, LANES)
            )

        def grad_in(h, _, b=b, rows=rows):
            cols = head_cols(h)
            r = b * heads + h
            inv = scale_col[b, 0]
            grad = (upstream(rows, cols, r) - attn[r] * inv * scale_col[b, 1]) * inv
            gattn[r] = grad
            back_state[r] = outer_state(q_ref[rows, cols], grad * carry[r])
            if b == blocks - 1:
                acc = back_state[r]
                prod = factor_of(b, h)
                for e in range(blocks - 2, -1, -1):
                    acc = factor_of(e, h) * acc + back_state[e * heads + h]
                    prod = prod * factor_of(e, h)
                begin(1, h, acc, prod)
            return 0

        lax.fori_loop(0, heads, grad_in, 0)

    def retreat(h, _):
        cols = head_cols(h)
        for b in range(blocks):
            r = b * heads + h
            rows = block_rows(b)
            query, key, value = q_ref[rows, cols], k_ref[rows, cols], v_ref[rows, cols]
            normed = attn[r] * scale_col[b, 0]
            gate = sig[r]
            gated = normed * (gain_ref[:, cols] * gate)
            att_ref[rows, cols] = gated.astype(BF16)
            dg_ref[rows, cols] = (cot_ref[rows, cols].astype(F32) * gated * (1.0 - gate)).astype(BF16)
            high, low = split(gattn[r])
            state_high, state_low = split(states[r])
            crossed = mm_rt(
                jnp.concatenate([high, low], axis=1),
                jnp.concatenate([state_high, state_high], axis=1),
            ) + mm_rt(high, state_low)
            crossed = carry[r] * crossed
            back = []
            for top, bottom in ((0, HALF), (HALF, BLOCK)):
                scores = mm_rt(high[top:bottom], value[:bottom])
                piece = (scores * within[r, top:bottom, :bottom]).astype(BF16)
                back.append(piece)
                dq_ref[pl.ds(b * BLOCK + top, HALF), cols] = (
                    mm(piece, key[:bottom]) + crossed[top:bottom]
                ).astype(BF16)
            key_acc[r] = mm_lt(back[1], query[HALF:])
            key_acc[r, :HALF, :] += mm_lt(back[0], query[:HALF])
            value_acc[r] = mm_lt(weights[r, HALF:, :], high[HALF:])
            value_acc[r, :HALF, :] += mm_lt(weights[r, :HALF, :HALF], high[:HALF])
        if steps > 1:
            advance(1, 0, h)
        return 0

    lax.fori_loop(0, heads, retreat, 0)
    advance_rest(1)
    if steps > 0:
        for h in range(heads):
            advance(1, steps - 1, h)


def finish_kernel(
    heads, blocks,
    k_ref, v_ref, att_in, dq_in, dg_in, key_acc, value_acc, last, factor, back_state, prefix,
    att_out, dq_out, dk_out, dv_out, dg_out,
    dk_ref, dv_ref, coming_ref, ready_sem, block_sem,
):
    ready = [
        pltpu.make_async_copy(src, dst, ready_sem.at[i])
        for i, (src, dst) in enumerate(((att_in, att_out), (dq_in, dq_out), (dg_in, dg_out)))
    ]
    for copy in ready:
        copy.start()
    for h in range(heads):
        coming_ref[h] = prefix[h, :D_HEAD, :]
    for b in range(blocks - 1, -1, -1):
        rows = pl.ds(b * BLOCK, BLOCK)

        def finish(h, _, b=b, rows=rows):
            cols = pl.ds(pl.multiple_of(h * D_HEAD, D_HEAD), D_HEAD)
            r = b * heads + h
            coming = coming_ref[h]
            dk_ref[rows, cols] = (
                key_acc[r] + last[r] * times_state_t(v_ref[rows, cols], coming)
            ).astype(BF16)
            dv_ref[rows, cols] = (
                value_acc[r] + last[r] * times_state(k_ref[rows, cols], coming)
            ).astype(BF16)
            coming_ref[h] = factor[pl.ds(r, 1), :] * coming + back_state[r]
            return 0

        lax.fori_loop(0, heads, finish, 0)
        for i, (src, dst) in enumerate(((dk_ref, dk_out), (dv_ref, dv_out))):
            copy = pltpu.make_async_copy(src.at[rows, :], dst.at[rows, :], block_sem.at[b, i])
            copy.start()
            ready.append(copy)
    for copy in ready:
        copy.wait()


def local(ctx_count, tp_count, query_rows, key_rows, value_rows, gate_logits, norm_gain, log_decay,
          offsets, cotangent):
    heads = log_decay.shape[0]
    tokens, width = query_rows.shape
    blocks = tokens // BLOCK
    count = heads * blocks
    steps = (ctx_count - 1).bit_length()
    out = jax.ShapeDtypeStruct((tokens, width), BF16)
    vmem = pl.BlockSpec(memory_space=pltpu.VMEM)
    anywhere = pl.BlockSpec(memory_space=pl.ANY)
    tile = (count, BLOCK, LANES)
    state = (count, D_HEAD, D_HEAD)
    message = (heads, D_HEAD + 8, LANES)
    held = pl.pallas_call(
        functools.partial(kernel, ctx_count, tp_count, heads, blocks),
        out_shape=(
            pltpu.VMEM((tokens, width), BF16),
            pltpu.VMEM((tokens, width), BF16),
            pltpu.VMEM((tokens, width), BF16),
            pltpu.VMEM(tile, F32),
            pltpu.VMEM(tile, F32),
            pltpu.VMEM(tile, F32),
            pltpu.VMEM((count, LANES), F32),
            pltpu.VMEM(state, F32),
            pltpu.VMEM(message, F32),
        ),
        in_specs=[pl.BlockSpec(memory_space=pltpu.SMEM)] + [anywhere] * 4 + [vmem] * 2 + [anywhere],
        out_specs=(vmem,) * 9,
        scratch_shapes=[
            pltpu.VMEM((count, BLOCK), F32),
            pltpu.VMEM(tile, F32),
            pltpu.VMEM(tile, F32),
            pltpu.VMEM((blocks, BLOCK, BLOCK), F32),
            pltpu.VMEM((count, BLOCK, BLOCK), F32),
            pltpu.VMEM((count, BLOCK, BLOCK), BF16),
            pltpu.VMEM(tile, F32),
            pltpu.VMEM(tile, F32),
            pltpu.VMEM(tile, F32),
            pltpu.VMEM(state, F32),
            pltpu.VMEM(state, F32),
            pltpu.VMEM(message, F32),
            pltpu.VMEM((2, steps) + message, F32),
            pltpu.VMEM((2, steps) + message, F32),
            pltpu.VMEM((blocks, 8, LANES), F32),
            pltpu.VMEM((blocks, tp_count - 1, 8, LANES), F32),
            pltpu.VMEM((blocks, 2, BLOCK, LANES), F32),
            pltpu.VMEM((tokens, width), BF16),
            pltpu.VMEM((tokens, width), BF16),
            pltpu.VMEM((tokens, width), BF16),
            pltpu.VMEM((tokens, width), BF16),
            pltpu.VMEM((tokens, width), BF16),
            pltpu.SemaphoreType.DMA((2, steps, heads)),
            pltpu.SemaphoreType.DMA((2, steps, heads)),
            pltpu.SemaphoreType.DMA((blocks, tp_count - 1)),
            pltpu.SemaphoreType.DMA((blocks, tp_count - 1)),
            pltpu.SemaphoreType.DMA((5,)),
        ],
        compiler_params=pltpu.CompilerParams(
            collective_id=0, has_side_effects=True, vmem_limit_bytes=44 * 1024 * 1024
        ),
    )(
        offsets, query_rows, key_rows, value_rows, gate_logits,
        norm_gain.reshape(1, width), log_decay, cotangent,
    )
    return pl.pallas_call(
        functools.partial(finish_kernel, heads, blocks),
        out_shape=(out,) * 5,
        in_specs=[vmem] * 11,
        out_specs=(anywhere,) * 5,
        scratch_shapes=[
            pltpu.VMEM((tokens, width), BF16),
            pltpu.VMEM((tokens, width), BF16),
            pltpu.VMEM((heads, D_HEAD, LANES), F32),
            pltpu.SemaphoreType.DMA((3,)),
            pltpu.SemaphoreType.DMA((blocks, 2)),
        ],
        compiler_params=pltpu.CompilerParams(vmem_limit_bytes=24 * 1024 * 1024),
    )(key_rows, value_rows, *held)


def solution(mesh):
    rows = P("ctx", "tp")
    return jax.shard_map(
        functools.partial(local, mesh.shape["ctx"], mesh.shape["tp"]),
        mesh=mesh,
        in_specs=(rows, rows, rows, rows, P("tp"), P("tp", "ctx"), P(), rows),
        out_specs=(rows,) * 5,
        check_vma=False,
    )
```

```python
import functools

import jax
import jax.numpy as jnp
from jax import lax
from jax.experimental import pallas as pl
from jax.experimental.pallas import tpu as pltpu
from jax.sharding import PartitionSpec as P

D_HEAD = 128
BLOCK = 512
HALF = 256
LANES = 128
EPS_NORM = 1e-06
MASKED = -1000.0
MESH = pl.DeviceIdType.MESH
F32 = jnp.float32
BF16 = jnp.bfloat16


def split(value):
    high = value.astype(BF16)
    return high, (value - high.astype(F32)).astype(BF16)


def dot(left, right, dims):
    return lax.dot_general(left, right, (dims, ((), ())), preferred_element_type=F32)


def mm(left, right):
    return dot(left, right, ((1,), (0,)))


def mm_rt(left, right):
    return dot(left, right, ((1,), (1,)))


def mm_lt(left, right):
    return dot(left, right, ((0,), (0,)))


def times_state(rows, state):
    return mm(jnp.concatenate([rows, rows], axis=1), jnp.concatenate(split(state), axis=0))


def times_state_t(rows, state):
    return mm_rt(jnp.concatenate([rows, rows], axis=1), jnp.concatenate(split(state), axis=1))


def outer_state(rows, weighted):
    both = mm_lt(rows, jnp.concatenate(split(weighted), axis=1))
    return both[:, :D_HEAD] + both[:, D_HEAD:]


def kernel(
    ctx_count, tp_count, heads, blocks,
    offs_hbm, q_hbm, k_hbm, v_hbm, gate_hbm, gain_hbm, decay_hbm, cot_hbm,
    att_ref, dq_ref, dg_ref, key_acc, value_acc, last, factor, back_state, prefix,
    run_row, run_col, carry, bias, within, weights,
    attn, sig, gattn, states, local_state,
    total, send_state, recv_state, sums, recv_sums, scale_col,
    offs, q_ref, k_ref, v_ref, gate_ref, gain_ref, decay_ref, cot_ref,
    send_sem, recv_sem, sum_send_sem, sum_recv_sem, load_sem,
):
    loads = [
        pltpu.make_async_copy(src, dst, load_sem.at[i])
        for i, (src, dst) in enumerate((
            (decay_hbm, decay_ref), (offs_hbm, offs), (k_hbm, k_ref), (v_hbm, v_ref),
            (q_hbm, q_ref), (gate_hbm, gate_ref), (cot_hbm, cot_ref), (gain_hbm, gain_ref),
        ))
    ]
    for load in loads:
        load.start()
    ctx = lax.axis_index("ctx")
    tp = lax.axis_index("tp")
    steps = (ctx_count - 1).bit_length()
    features = tp_count * heads * D_HEAD
    offset_count = offs.shape[0]

    def partner(step):
        size = 1 << step
        return ctx + size * (1 - 2 * ((ctx // size) % 2))

    def peer(hop):
        return lax.rem(tp + hop, tp_count)

    barrier = pltpu.get_barrier_semaphore()
    for step in range(steps):
        pl.semaphore_signal(barrier, inc=1, device_id=(partner(step), tp), device_id_type=MESH)
    for hop in range(1, tp_count):
        pl.semaphore_signal(barrier, inc=1, device_id=(ctx, peer(hop)), device_id_type=MESH)

    first = ctx * (blocks * BLOCK)

    def segment(positions):
        count = (offs[0] <= positions).astype(jnp.int32)
        for entry in range(1, offset_count):
            count = count + (offs[entry] <= positions).astype(jnp.int32)
        return count

    loads[0].wait()
    loads[1].wait()
    decays = jnp.concatenate(
        [decay_ref[:, b * BLOCK:(b + 1) * BLOCK] for b in range(blocks)], axis=0
    )
    rest = decays
    pieces = []
    for _ in range(3):
        piece = rest.astype(BF16)
        pieces.append(piece)
        rest = rest - piece.astype(F32)
    lower = lax.broadcasted_iota(jnp.int32, (BLOCK, BLOCK), 0)
    upper = lax.broadcasted_iota(jnp.int32, (BLOCK, BLOCK), 1)
    summing = jnp.where(lower <= upper, 1.0, 0.0).astype(BF16)
    running = mm(pieces[2], summing) + mm(pieces[1], summing) + mm(pieces[0], summing)
    run_row[...] = running
    lane = lax.broadcasted_iota(jnp.int32, (1, BLOCK), 1)
    sub = lax.broadcasted_iota(jnp.int32, (BLOCK, 1), 0)
    carry_rows, last_rows = [], []
    for b in range(blocks):
        start = first + b * BLOCK
        rows = running[b * heads:(b + 1) * heads]
        seg_row = segment(start + lane)
        seg_col = segment(start + sub)
        before = segment(start - 1)
        final = segment(start + BLOCK - 1)
        bias[b] = jnp.where((seg_col == seg_row) & (lower >= upper), 0.0, MASKED)
        carry_rows.append(jnp.where(seg_row == before, jnp.exp(rows), 0.0))
        end = rows[:, BLOCK - 1:]
        last_rows.append(jnp.where(seg_row == final, jnp.exp(jnp.minimum(end - rows, 0.0)), 0.0))
        whole = jnp.where(before == final, jnp.exp(end), 0.0)
        factor[b * heads:(b + 1) * heads, :] = jnp.broadcast_to(whole, (heads, LANES))
    count = heads * blocks
    stacked = jnp.concatenate(
        [running] + carry_rows + last_rows + [jnp.zeros((LANES - 3 * count, BLOCK), F32)], axis=0
    )
    columns = stacked.T
    for r in range(count):
        run_col[r] = jnp.broadcast_to(columns[:, r:r + 1], (BLOCK, LANES))
        carry[r] = jnp.broadcast_to(columns[:, count + r:count + r + 1], (BLOCK, LANES))
        last[r] = jnp.broadcast_to(columns[:, 2 * count + r:2 * count + r + 1], (BLOCK, LANES))

    def head_cols(h):
        return pl.ds(pl.multiple_of(h * D_HEAD, D_HEAD), D_HEAD)

    def block_rows(b):
        return pl.ds(b * BLOCK, BLOCK)

    def factor_of(b, h):
        return factor[pl.ds(b * heads + h, 1), :]

    def exchange(way, step, h):
        return pltpu.make_async_remote_copy(
            src_ref=send_state.at[way, step, h],
            dst_ref=recv_state.at[way, step, h],
            send_sem=send_sem.at[way, step, h],
            recv_sem=recv_sem.at[way, step, h],
            device_id=(partner(step), tp),
            device_id_type=MESH,
        )

    def begin(way, h, state, state_factor):
        prefix[h, :D_HEAD, :] = jnp.zeros((D_HEAD, LANES), F32)
        prefix[h, D_HEAD:, :] = jnp.ones((8, LANES), F32)
        spread = jnp.broadcast_to(state_factor, (8, LANES))
        total[h, :D_HEAD, :] = state
        total[h, D_HEAD:, :] = spread
        send_state[way, 0, h, :D_HEAD, :] = state
        send_state[way, 0, h, D_HEAD:, :] = spread
        exchange(way, 0, h).start()

    def advance(way, step, h):
        exchange(way, step, h).wait()
        size = 1 << step
        bit = (ctx // size) % 2
        after = bit == 1 if way == 0 else bit == 0
        other = recv_state[way, step, h, :D_HEAD, :]
        other_factor = recv_state[way, step, h, D_HEAD:, :][:1]
        mine = total[h, :D_HEAD, :]
        my_factor = total[h, D_HEAD:, :][:1]
        if step + 1 < steps:
            joined = jnp.where(after, my_factor * other + mine, other_factor * mine + other)
            spread = jnp.broadcast_to(my_factor * other_factor, (8, LANES))
            send_state[way, step + 1, h, :D_HEAD, :] = joined
            send_state[way, step + 1, h, D_HEAD:, :] = spread
            exchange(way, step + 1, h).start()
            total[h, :D_HEAD, :] = joined
            total[h, D_HEAD:, :] = spread
        so_far = prefix[h, :D_HEAD, :]
        so_far_factor = prefix[h, D_HEAD:, :][:1]
        prefix[h, :D_HEAD, :] = jnp.where(after, so_far_factor * other + so_far, so_far)
        prefix[h, D_HEAD:, :] = jnp.broadcast_to(
            jnp.where(after, so_far_factor * other_factor, so_far_factor), (8, LANES)
        )

    def join_early(way, h):
        if steps > 1:
            @pl.when(h > 0)
            def _():
                advance(way, 0, h - 1)

            @pl.when(h == heads - 1)
            def _():
                advance(way, 0, h)

    def advance_rest(way):
        for step in range(1, steps - 1):
            for h in range(heads):
                advance(way, step, h)

    pl.semaphore_wait(barrier, steps + tp_count - 1)
    loads[2].wait()
    loads[3].wait()

    def summarize(h, _):
        cols = head_cols(h)
        acc = None
        prod = None
        for b in range(blocks):
            r = b * heads + h
            weighted = v_ref[block_rows(b), cols].astype(F32) * last[r]
            state = outer_state(k_ref[block_rows(b), cols], weighted)
            local_state[r] = state
            fac = factor_of(b, h)
            acc = state if acc is None else fac * acc + state
            prod = fac if prod is None else prod * fac
        begin(0, h, acc, prod)
        return 0

    lax.fori_loop(0, heads, summarize, 0, unroll=True)

    loads[4].wait()
    loads[5].wait()
    def attend(h, _):
        cols = head_cols(h)
        join_early(0, h)
        for b in range(blocks):
            r = b * heads + h
            rows = block_rows(b)
            query, key, value = q_ref[rows, cols], k_ref[rows, cols], v_ref[rows, cols]
            for top, bottom in ((0, HALF), (HALF, BLOCK)):
                col = run_col[r, top:bottom, :]
                col = jnp.concatenate([col] * (bottom // LANES), axis=1)
                row = run_row[pl.ds(r, 1), :][:, :bottom]
                decay = jnp.exp(jnp.minimum(col - row, bias[b, top:bottom, :bottom]))
                within[r, top:bottom, :bottom] = decay
                scores = mm_rt(query[top:bottom], key[:bottom])
                weight = (scores * decay).astype(BF16)
                weights[r, top:bottom, :bottom] = weight
                attn[r, top:bottom, :] = mm(weight, value[:bottom])
            sig[r] = jax.nn.sigmoid(gate_ref[rows, cols].astype(F32))
        return 0

    lax.fori_loop(0, heads, attend, 0, unroll=True)
    advance_rest(0)
    loads[6].wait()
    loads[7].wait()

    def sum_copy(b, hop):
        return pltpu.make_async_remote_copy(
            src_ref=sums.at[b],
            dst_ref=recv_sums.at[b, hop - 1],
            send_sem=sum_send_sem.at[b, hop - 1],
            recv_sem=sum_recv_sem.at[b, hop - 1],
            device_id=(ctx, peer(hop)),
            device_id_type=MESH,
        )

    def upstream(rows, cols, r):
        return cot_ref[rows, cols].astype(F32) * (gain_ref[:, cols] * sig[r])

    ones = jnp.ones((8, 2 * LANES), BF16)
    chunks = BLOCK // LANES
    for b in range(blocks):
        rows = block_rows(b)

        def carry_in(h, acc, b=b, rows=rows):
            cols = head_cols(h)
            r = b * heads + h
            if b == 0 and steps > 0:
                advance(0, steps - 1, h)
            state = prefix[h, :D_HEAD, :]
            states[r] = state
            value = attn[r] + carry[r] * times_state(q_ref[rows, cols], state)
            attn[r] = value
            prefix[h, :D_HEAD, :] = factor_of(b, h) * state + local_state[r]
            return acc[0] + value * value, acc[1] + upstream(rows, cols, r) * value

        zero = jnp.zeros((BLOCK, LANES), F32)
        squares, inners = lax.fori_loop(0, heads, carry_in, (zero, zero), unroll=True)
        for at, part in ((0, squares), (chunks, inners)):
            line = mm_rt(ones, jnp.concatenate(split(part), axis=1))
            for c in range(chunks):
                sums[b, at + c:at + c + 1, :] = line[:1, c * LANES:(c + 1) * LANES]
        for hop in range(1, tp_count):
            sum_copy(b, hop).start()

    for b in range(blocks):
        rows = block_rows(b)
        added = sums[b]
        for hop in range(1, tp_count):
            sum_copy(b, hop).wait()
            added = added + recv_sums[b, hop - 1]
        inverse = 1.0 / jnp.sqrt(added[:chunks] / features + EPS_NORM)
        mean_inner = added[chunks:] * inverse / features
        turned = jnp.concatenate(
            [inverse, mean_inner, jnp.zeros((LANES - 2 * chunks, LANES), F32)], axis=0
        ).T
        for c in range(chunks):
            here = pl.ds(c * LANES, LANES)
            scale_col[b, 0, here, :] = jnp.broadcast_to(turned[:, c:c + 1], (LANES, LANES))
            scale_col[b, 1, here, :] = jnp.broadcast_to(
                turned[:, chunks + c:chunks + c + 1], (LANES, LANES)
            )

        def grad_in(h, _, b=b, rows=rows):
            cols = head_cols(h)
            r = b * heads + h
            inv = scale_col[b, 0]
            grad = (upstream(rows, cols, r) - attn[r] * inv * scale_col[b, 1]) * inv
            gattn[r] = grad
            back_state[r] = outer_state(q_ref[rows, cols], grad * carry[r])
            if b == blocks - 1:
                acc = back_state[r]
                prod = factor_of(b, h)
                for e in range(blocks - 2, -1, -1):
                    acc = factor_of(e, h) * acc + back_state[e * heads + h]
                    prod = prod * factor_of(e, h)
                begin(1, h, acc, prod)
            return 0

        lax.fori_loop(0, heads, grad_in, 0, unroll=True)

    def retreat(h, _):
        cols = head_cols(h)
        join_early(1, h)
        for b in range(blocks):
            r = b * heads + h
            rows = block_rows(b)
            query, key, value = q_ref[rows, cols], k_ref[rows, cols], v_ref[rows, cols]
            normed = attn[r] * scale_col[b, 0]
            gate = sig[r]
            gated = normed * (gain_ref[:, cols] * gate)
            att_ref[rows, cols] = gated.astype(BF16)
            dg_ref[rows, cols] = (cot_ref[rows, cols].astype(F32) * gated * (1.0 - gate)).astype(BF16)
            high, low = split(gattn[r])
            state_high, state_low = split(states[r])
            crossed = mm_rt(
                jnp.concatenate([high, low], axis=1),
                jnp.concatenate([state_high, state_high], axis=1),
            ) + mm_rt(high, state_low)
            crossed = carry[r] * crossed
            back = []
            for top, bottom in ((0, HALF), (HALF, BLOCK)):
                scores = mm_rt(high[top:bottom], value[:bottom])
                piece = (scores * within[r, top:bottom, :bottom]).astype(BF16)
                back.append(piece)
                dq_ref[pl.ds(b * BLOCK + top, HALF), cols] = (
                    mm(piece, key[:bottom]) + crossed[top:bottom]
                ).astype(BF16)
            key_acc[r] = mm_lt(back[1], query[HALF:])
            key_acc[r, :HALF, :] += mm_lt(back[0], query[:HALF])
            value_acc[r] = mm_lt(weights[r, HALF:, :], high[HALF:])
            value_acc[r, :HALF, :] += mm_lt(weights[r, :HALF, :HALF], high[:HALF])
        return 0

    lax.fori_loop(0, heads, retreat, 0, unroll=True)
    advance_rest(1)
    if steps > 0:
        for h in range(heads):
            advance(1, steps - 1, h)


def finish_kernel(
    heads, blocks,
    k_ref, v_ref, att_in, dq_in, dg_in, key_acc, value_acc, last, factor, back_state, prefix,
    att_out, dq_out, dk_out, dv_out, dg_out,
    dk_ref, dv_ref, coming_ref, ready_sem, block_sem,
):
    ready = [
        pltpu.make_async_copy(src, dst, ready_sem.at[i])
        for i, (src, dst) in enumerate(((att_in, att_out), (dq_in, dq_out), (dg_in, dg_out)))
    ]
    for copy in ready:
        copy.start()
    for h in range(heads):
        coming_ref[h] = prefix[h, :D_HEAD, :]
    for b in range(blocks - 1, -1, -1):
        rows = pl.ds(b * BLOCK, BLOCK)

        def finish(h, _, b=b, rows=rows):
            cols = pl.ds(pl.multiple_of(h * D_HEAD, D_HEAD), D_HEAD)
            r = b * heads + h
            coming = coming_ref[h]
            dk_ref[rows, cols] = (
                key_acc[r] + last[r] * times_state_t(v_ref[rows, cols], coming)
            ).astype(BF16)
            dv_ref[rows, cols] = (
                value_acc[r] + last[r] * times_state(k_ref[rows, cols], coming)
            ).astype(BF16)
            coming_ref[h] = factor[pl.ds(r, 1), :] * coming + back_state[r]
            return 0

        lax.fori_loop(0, heads, finish, 0, unroll=True)
        for i, (src, dst) in enumerate(((dk_ref, dk_out), (dv_ref, dv_out))):
            copy = pltpu.make_async_copy(src.at[rows, :], dst.at[rows, :], block_sem.at[b, i])
            copy.start()
            ready.append(copy)
    for copy in ready:
        copy.wait()


def local(ctx_count, tp_count, query_rows, key_rows, value_rows, gate_logits, norm_gain, log_decay,
          offsets, cotangent):
    heads = log_decay.shape[0]
    tokens, width = query_rows.shape
    blocks = tokens // BLOCK
    count = heads * blocks
    steps = (ctx_count - 1).bit_length()
    out = jax.ShapeDtypeStruct((tokens, width), BF16)
    vmem = pl.BlockSpec(memory_space=pltpu.VMEM)
    anywhere = pl.BlockSpec(memory_space=pl.ANY)
    tile = (count, BLOCK, LANES)
    state = (count, D_HEAD, D_HEAD)
    message = (heads, D_HEAD + 8, LANES)
    held = pl.pallas_call(
        functools.partial(kernel, ctx_count, tp_count, heads, blocks),
        out_shape=(
            pltpu.VMEM((tokens, width), BF16),
            pltpu.VMEM((tokens, width), BF16),
            pltpu.VMEM((tokens, width), BF16),
            pltpu.VMEM(tile, F32),
            pltpu.VMEM(tile, F32),
            pltpu.VMEM(tile, F32),
            pltpu.VMEM((count, LANES), F32),
            pltpu.VMEM(state, F32),
            pltpu.VMEM(message, F32),
        ),
        in_specs=[pl.BlockSpec(memory_space=pltpu.HBM)] * 8,
        out_specs=(vmem,) * 9,
        scratch_shapes=[
            pltpu.VMEM((count, BLOCK), F32),
            pltpu.VMEM(tile, F32),
            pltpu.VMEM(tile, F32),
            pltpu.VMEM((blocks, BLOCK, BLOCK), F32),
            pltpu.VMEM((count, BLOCK, BLOCK), F32),
            pltpu.VMEM((count, BLOCK, BLOCK), BF16),
            pltpu.VMEM(tile, F32),
            pltpu.VMEM(tile, F32),
            pltpu.VMEM(tile, F32),
            pltpu.VMEM(state, F32),
            pltpu.VMEM(state, F32),
            pltpu.VMEM(message, F32),
            pltpu.VMEM((2, steps) + message, F32),
            pltpu.VMEM((2, steps) + message, F32),
            pltpu.VMEM((blocks, 8, LANES), F32),
            pltpu.VMEM((blocks, tp_count - 1, 8, LANES), F32),
            pltpu.VMEM((blocks, 2, BLOCK, LANES), F32),
            pltpu.SMEM(offsets.shape, jnp.int32),
            pltpu.VMEM((tokens, width), BF16),
            pltpu.VMEM((tokens, width), BF16),
            pltpu.VMEM((tokens, width), BF16),
            pltpu.VMEM((tokens, width), BF16),
            pltpu.VMEM((1, width), F32),
            pltpu.VMEM(log_decay.shape, F32),
            pltpu.VMEM((tokens, width), BF16),
            pltpu.SemaphoreType.DMA((2, steps, heads)),
            pltpu.SemaphoreType.DMA((2, steps, heads)),
            pltpu.SemaphoreType.DMA((blocks, tp_count - 1)),
            pltpu.SemaphoreType.DMA((blocks, tp_count - 1)),
            pltpu.SemaphoreType.DMA((8,)),
        ],
        compiler_params=pltpu.CompilerParams(
            collective_id=0, has_side_effects=True, vmem_limit_bytes=44 * 1024 * 1024
        ),
    )(*[
        pltpu.with_memory_space_constraint(array, pltpu.HBM)
        for array in (
            offsets, query_rows, key_rows, value_rows, gate_logits,
            norm_gain.reshape(1, width), log_decay, cotangent,
        )
    ])
    return pl.pallas_call(
        functools.partial(finish_kernel, heads, blocks),
        out_shape=(out,) * 5,
        in_specs=[vmem] * 11,
        out_specs=(anywhere,) * 5,
        scratch_shapes=[
            pltpu.VMEM((tokens, width), BF16),
            pltpu.VMEM((tokens, width), BF16),
            pltpu.VMEM((heads, D_HEAD, LANES), F32),
            pltpu.SemaphoreType.DMA((3,)),
            pltpu.SemaphoreType.DMA((blocks, 2)),
        ],
        compiler_params=pltpu.CompilerParams(vmem_limit_bytes=24 * 1024 * 1024),
    )(key_rows, value_rows, *held)


def solution(mesh):
    rows = P("ctx", "tp")
    return jax.shard_map(
        functools.partial(local, mesh.shape["ctx"], mesh.shape["tp"]),
        mesh=mesh,
        in_specs=(rows, rows, rows, rows, P("tp"), P("tp", "ctx"), P(), rows),
        out_specs=(rows,) * 5,
        check_vma=False,
    )
```

```python
import functools

import jax
import jax.numpy as jnp
from jax import lax
from jax.experimental import pallas as pl
from jax.experimental.pallas import tpu as pltpu
from jax.sharding import PartitionSpec as P

D_HEAD = 128
BLOCK = 512
HALF = 256
LANES = 128
EPS_NORM = 1e-06
MASKED = -1000.0
MESH = pl.DeviceIdType.MESH
F32 = jnp.float32
BF16 = jnp.bfloat16


def split(value):
    high = value.astype(BF16)
    return high, (value - high.astype(F32)).astype(BF16)


def dot(left, right, dims):
    return lax.dot_general(left, right, (dims, ((), ())), preferred_element_type=F32)


def mm(left, right):
    return dot(left, right, ((1,), (0,)))


def mm_rt(left, right):
    return dot(left, right, ((1,), (1,)))


def twice(rows):
    return jnp.concatenate([rows, rows], axis=0)


def state_times(state, columns):
    return mm(jnp.concatenate(split(state), axis=1), twice(columns))


def outer_state(columns, weighted):
    both = mm_rt(columns, jnp.concatenate(split(weighted), axis=0))
    return both[:, :D_HEAD] + both[:, D_HEAD:]


def causal(left, right, product):
    first = product(left[:, :HALF], right[0])
    second = product(left[:, HALF:], right[1])
    return jnp.concatenate([first[:, :HALF], first[:, HALF:] + second], axis=1)


def kernel(
    ctx_count, tp_count, heads, blocks,
    offs_hbm, q_hbm, k_hbm, v_hbm, gate_hbm, gain_hbm, decay_hbm, cot_hbm,
    att_ref, dq_ref, dg_ref, key_cols, value_cols, key_acc, value_acc, last, factor, back_state,
    prefix,
    run_row, run_col, carry, bias, within, weights,
    query_cols, gain_cols, attn, sig, upstream, gattn, states, local_state,
    total, send_state, recv_state, sums, recv_sums,
    offs, q_ref, k_ref, v_ref, gate_ref, gain_ref, decay_ref, cot_ref,
    send_sem, recv_sem, sum_send_sem, sum_recv_sem, load_sem,
):
    loads = [
        pltpu.make_async_copy(src, dst, load_sem.at[i])
        for i, (src, dst) in enumerate((
            (decay_hbm, decay_ref), (offs_hbm, offs), (k_hbm, k_ref), (v_hbm, v_ref),
            (q_hbm, q_ref), (gate_hbm, gate_ref), (cot_hbm, cot_ref), (gain_hbm, gain_ref),
        ))
    ]
    for load in loads:
        load.start()
    ctx = lax.axis_index("ctx")
    tp = lax.axis_index("tp")
    steps = (ctx_count - 1).bit_length()
    features = tp_count * heads * D_HEAD
    offset_count = offs.shape[0]

    def partner(step):
        size = 1 << step
        return ctx + size * (1 - 2 * ((ctx // size) % 2))

    def peer(hop):
        return lax.rem(tp + hop, tp_count)

    barrier = pltpu.get_barrier_semaphore()
    for step in range(steps):
        pl.semaphore_signal(barrier, inc=1, device_id=(partner(step), tp), device_id_type=MESH)
    for hop in range(1, tp_count):
        pl.semaphore_signal(barrier, inc=1, device_id=(ctx, peer(hop)), device_id_type=MESH)

    first = ctx * (blocks * BLOCK)

    def segment(positions):
        count = (offs[0] <= positions).astype(jnp.int32)
        for entry in range(1, offset_count):
            count = count + (offs[entry] <= positions).astype(jnp.int32)
        return count

    loads[0].wait()
    loads[1].wait()
    decays = jnp.concatenate(
        [decay_ref[:, b * BLOCK:(b + 1) * BLOCK] for b in range(blocks)], axis=0
    )
    rest = decays
    pieces = []
    for _ in range(3):
        piece = rest.astype(BF16)
        pieces.append(piece)
        rest = rest - piece.astype(F32)
    lower = lax.broadcasted_iota(jnp.int32, (BLOCK, BLOCK), 0)
    upper = lax.broadcasted_iota(jnp.int32, (BLOCK, BLOCK), 1)
    summing = jnp.where(lower <= upper, 1.0, 0.0).astype(BF16)
    running = mm(pieces[2], summing) + mm(pieces[1], summing) + mm(pieces[0], summing)
    run_row[...] = running
    lane = lax.broadcasted_iota(jnp.int32, (1, BLOCK), 1)
    sub = lax.broadcasted_iota(jnp.int32, (BLOCK, 1), 0)
    carry_rows, last_rows = [], []
    for b in range(blocks):
        start = first + b * BLOCK
        rows = running[b * heads:(b + 1) * heads]
        seg_row = segment(start + lane)
        seg_col = segment(start + sub)
        before = segment(start - 1)
        final = segment(start + BLOCK - 1)
        bias[b] = jnp.where((seg_col == seg_row) & (lower <= upper), 0.0, MASKED)
        carry_rows.append(jnp.where(seg_row == before, jnp.exp(rows), 0.0))
        end = rows[:, BLOCK - 1:]
        last_rows.append(jnp.where(seg_row == final, jnp.exp(jnp.minimum(end - rows, 0.0)), 0.0))
        whole = jnp.where(before == final, jnp.exp(end), 0.0)
        factor[b * heads:(b + 1) * heads, :] = jnp.broadcast_to(whole, (heads, LANES))
    count = heads * blocks
    carry[...] = jnp.concatenate(carry_rows, axis=0)
    last[...] = jnp.concatenate(last_rows, axis=0)
    columns = jnp.concatenate([running, jnp.zeros((LANES - count, BLOCK), F32)], axis=0).T
    for r in range(count):
        run_col[r] = jnp.broadcast_to(columns[:, r:r + 1], (BLOCK, LANES))

    def head_cols(h):
        return pl.ds(pl.multiple_of(h * D_HEAD, D_HEAD), D_HEAD)

    def block_rows(b):
        return pl.ds(b * BLOCK, BLOCK)

    def factor_of(b, h):
        return factor[pl.ds(b * heads + h, 1), :]

    def exchange(way, step, h):
        return pltpu.make_async_remote_copy(
            src_ref=send_state.at[way, step, h],
            dst_ref=recv_state.at[way, step, h],
            send_sem=send_sem.at[way, step, h],
            recv_sem=recv_sem.at[way, step, h],
            device_id=(partner(step), tp),
            device_id_type=MESH,
        )

    def begin(way, h, state, state_factor):
        prefix[h, :D_HEAD, :] = jnp.zeros((D_HEAD, LANES), F32)
        prefix[h, D_HEAD:, :] = jnp.ones((8, LANES), F32)
        spread = jnp.broadcast_to(state_factor, (8, LANES))
        total[h, :D_HEAD, :] = state
        total[h, D_HEAD:, :] = spread
        send_state[way, 0, h, :D_HEAD, :] = state
        send_state[way, 0, h, D_HEAD:, :] = spread
        exchange(way, 0, h).start()

    def advance(way, step, h):
        exchange(way, step, h).wait()
        size = 1 << step
        bit = (ctx // size) % 2
        after = bit == 1 if way == 0 else bit == 0
        other = recv_state[way, step, h, :D_HEAD, :]
        other_factor = recv_state[way, step, h, D_HEAD:, :][:1]
        mine = total[h, :D_HEAD, :]
        my_factor = total[h, D_HEAD:, :][:1]
        if step + 1 < steps:
            joined = jnp.where(after, my_factor * other + mine, other_factor * mine + other)
            spread = jnp.broadcast_to(my_factor * other_factor, (8, LANES))
            send_state[way, step + 1, h, :D_HEAD, :] = joined
            send_state[way, step + 1, h, D_HEAD:, :] = spread
            exchange(way, step + 1, h).start()
            total[h, :D_HEAD, :] = joined
            total[h, D_HEAD:, :] = spread
        so_far = prefix[h, :D_HEAD, :]
        so_far_factor = prefix[h, D_HEAD:, :][:1]
        prefix[h, :D_HEAD, :] = jnp.where(after, so_far_factor * other + so_far, so_far)
        prefix[h, D_HEAD:, :] = jnp.broadcast_to(
            jnp.where(after, so_far_factor * other_factor, so_far_factor), (8, LANES)
        )

    def join_early(way, h):
        if steps > 1:
            @pl.when(h > 0)
            def _():
                advance(way, 0, h - 1)

            @pl.when(h == heads - 1)
            def _():
                advance(way, 0, h)

    def advance_rest(way):
        for step in range(1, steps - 1):
            for h in range(heads):
                advance(way, step, h)

    pl.semaphore_wait(barrier, steps + tp_count - 1)
    loads[2].wait()
    loads[3].wait()

    def summarize(h, _):
        cols = head_cols(h)
        acc = None
        prod = None
        for b in range(blocks):
            r = b * heads + h
            key = k_ref[block_rows(b), cols].T
            value = v_ref[block_rows(b), cols].T
            key_cols[r] = key
            value_cols[r] = value
            state = outer_state(value, key.astype(F32) * last[pl.ds(r, 1), :])
            local_state[r] = state
            fac = factor_of(b, h)
            acc = state if acc is None else fac * acc + state
            prod = fac if prod is None else prod * fac
        begin(0, h, acc, prod)
        return 0

    lax.fori_loop(0, heads, summarize, 0, unroll=True)

    for load in loads[4:]:
        load.wait()
    def attend(h, _):
        cols = head_cols(h)
        join_early(0, h)
        gain = jnp.broadcast_to(gain_ref[:, cols], (D_HEAD, LANES)).T
        gain_cols[h] = gain
        gain = jnp.concatenate([gain] * (BLOCK // LANES), axis=1)
        for b in range(blocks):
            r = b * heads + h
            rows = block_rows(b)
            query = q_ref[rows, cols].T
            query_cols[r] = query
            parts = []
            for top in (0, HALF):
                half = slice(top, top + HALF)
                col = run_col[r, half, :]
                col = jnp.concatenate([col] * ((BLOCK - top) // LANES), axis=1)
                row = run_row[pl.ds(r, 1), :][:, top:]
                decay = jnp.exp(jnp.minimum(row - col, bias[b, half, top:]))
                within[r, half, top:] = decay
                scores = mm(k_ref[pl.ds(b * BLOCK + top, HALF), cols], query[:, top:])
                weight = (scores * decay).astype(BF16)
                weights[r, half, top:] = weight
                parts.append(weight)
            attn[r] = causal(value_cols[r], parts, mm)
            gate = jax.nn.sigmoid(gate_ref[rows, cols].T.astype(F32))
            sig[r] = gate
            upstream[r] = cot_ref[rows, cols].T.astype(F32) * (gain * gate)
        return 0

    lax.fori_loop(0, heads, attend, 0, unroll=True)
    advance_rest(0)

    def sum_copy(b, hop):
        return pltpu.make_async_remote_copy(
            src_ref=sums.at[b],
            dst_ref=recv_sums.at[b, hop - 1],
            send_sem=sum_send_sem.at[b, hop - 1],
            recv_sem=sum_recv_sem.at[b, hop - 1],
            device_id=(ctx, peer(hop)),
            device_id_type=MESH,
        )

    chunks = BLOCK // LANES
    for b in range(blocks):
        def carry_in(h, acc, b=b):
            r = b * heads + h
            if b == 0 and steps > 0:
                advance(0, steps - 1, h)
            state = prefix[h, :D_HEAD, :]
            states[r] = state
            value = attn[r] + carry[pl.ds(r, 1), :] * state_times(state, query_cols[r])
            attn[r] = value
            prefix[h, :D_HEAD, :] = factor_of(b, h) * state + local_state[r]
            return (
                acc[0] + jnp.sum(value * value, axis=0, keepdims=True),
                acc[1] + jnp.sum(upstream[r] * value, axis=0, keepdims=True),
            )

        zero = jnp.zeros((1, BLOCK), F32)
        squares, inners = lax.fori_loop(0, heads, carry_in, (zero, zero), unroll=True)
        for at, line in ((0, squares), (chunks, inners)):
            for c in range(chunks):
                sums[b, at + c:at + c + 1, :] = line[:1, c * LANES:(c + 1) * LANES]
        for hop in range(1, tp_count):
            sum_copy(b, hop).start()

    scales = []
    for b in range(blocks):
        added = sums[b]
        for hop in range(1, tp_count):
            sum_copy(b, hop).wait()
            added = added + recv_sums[b, hop - 1]
        inverse = 1.0 / jnp.sqrt(added[:chunks] / features + EPS_NORM)
        mean_inner = added[chunks:] * inverse / features
        inv, mean_inner = (
            jnp.concatenate([part[c:c + 1] for c in range(chunks)], axis=1)
            for part in (inverse, mean_inner)
        )
        scales.append(inv)

        def grad_in(h, _, b=b, inv=inv, mean_inner=mean_inner):
            r = b * heads + h
            grad = (upstream[r] - attn[r] * (inv * mean_inner)) * inv
            gattn[r] = grad
            back_state[r] = outer_state(query_cols[r], grad * carry[pl.ds(r, 1), :])
            if b == blocks - 1:
                acc = back_state[r]
                prod = factor_of(b, h)
                for e in range(blocks - 2, -1, -1):
                    acc = factor_of(e, h) * acc + back_state[e * heads + h]
                    prod = prod * factor_of(e, h)
                begin(1, h, acc, prod)
            return 0

        lax.fori_loop(0, heads, grad_in, 0, unroll=True)

    def retreat(h, _):
        cols = head_cols(h)
        join_early(1, h)
        gain = jnp.concatenate([gain_cols[h]] * (BLOCK // LANES), axis=1)
        for b in range(blocks):
            r = b * heads + h
            rows = block_rows(b)
            high, low = split(gattn[r])
            parts = []
            for top in (0, HALF):
                half = slice(top, top + HALF)
                scores = mm(v_ref[pl.ds(b * BLOCK + top, HALF), cols], high[:, top:])
                parts.append((scores * within[r, half, top:]).astype(BF16))
            state_high, state_low = split(states[r].T)
            crossed = mm(
                jnp.concatenate([state_high, state_high], axis=1),
                jnp.concatenate([high, low], axis=0),
            ) + mm(state_low, high)
            dq = causal(key_cols[r], parts, mm) + carry[pl.ds(r, 1), :] * crossed
            dq_ref[rows, cols] = dq.astype(BF16).T
            query = query_cols[r]
            key_acc[r, :, :HALF] = mm_rt(query, parts[0])
            key_acc[r, :, HALF:] = mm_rt(query[:, HALF:], parts[1])
            value_acc[r, :, :HALF] = mm_rt(high, weights[r, :HALF, :])
            value_acc[r, :, HALF:] = mm_rt(high[:, HALF:], weights[r, HALF:, HALF:])
            normed = attn[r] * scales[b]
            gate = sig[r]
            att_ref[rows, cols] = (normed * (gain * gate)).astype(BF16).T
            dg_ref[rows, cols] = (upstream[r] * normed * (1.0 - gate)).astype(BF16).T
        return 0

    lax.fori_loop(0, heads, retreat, 0, unroll=True)
    advance_rest(1)
    if steps > 0:
        for h in range(heads):
            advance(1, steps - 1, h)


def finish_kernel(
    heads, blocks,
    att_in, dq_in, dg_in, key_cols, value_cols, key_acc, value_acc, last, factor, back_state,
    prefix,
    att_out, dq_out, dk_out, dv_out, dg_out,
    dk_ref, dv_ref, coming_ref, ready_sem, block_sem,
):
    ready = [
        pltpu.make_async_copy(src, dst, ready_sem.at[i])
        for i, (src, dst) in enumerate(((att_in, att_out), (dq_in, dq_out), (dg_in, dg_out)))
    ]
    for copy in ready:
        copy.start()
    for h in range(heads):
        coming_ref[h] = prefix[h, :D_HEAD, :]
    for b in range(blocks - 1, -1, -1):
        rows = pl.ds(b * BLOCK, BLOCK)

        def finish(h, _, b=b, rows=rows):
            cols = pl.ds(pl.multiple_of(h * D_HEAD, D_HEAD), D_HEAD)
            r = b * heads + h
            coming = coming_ref[h]
            weight = last[pl.ds(r, 1), :]
            dk = key_acc[r] + weight * state_times(coming, value_cols[r])
            dv = value_acc[r] + weight * state_times(coming.T, key_cols[r])
            dk_ref[rows, cols] = dk.astype(BF16).T
            dv_ref[rows, cols] = dv.astype(BF16).T
            coming_ref[h] = factor[pl.ds(r, 1), :] * coming + back_state[r]
            return 0

        lax.fori_loop(0, heads, finish, 0, unroll=True)
        for i, (src, dst) in enumerate(((dk_ref, dk_out), (dv_ref, dv_out))):
            copy = pltpu.make_async_copy(src.at[rows, :], dst.at[rows, :], block_sem.at[b, i])
            copy.start()
            ready.append(copy)
    for copy in ready:
        copy.wait()


def local(ctx_count, tp_count, query_rows, key_rows, value_rows, gate_logits, norm_gain, log_decay,
          offsets, cotangent):
    heads = log_decay.shape[0]
    tokens, width = query_rows.shape
    blocks = tokens // BLOCK
    count = heads * blocks
    steps = (ctx_count - 1).bit_length()
    out = jax.ShapeDtypeStruct((tokens, width), BF16)
    vmem = pl.BlockSpec(memory_space=pltpu.VMEM)
    anywhere = pl.BlockSpec(memory_space=pl.ANY)
    tile = (count, D_HEAD, BLOCK)
    state = (count, D_HEAD, D_HEAD)
    message = (heads, D_HEAD + 8, LANES)
    held = pl.pallas_call(
        functools.partial(kernel, ctx_count, tp_count, heads, blocks),
        out_shape=(
            pltpu.VMEM((tokens, width), BF16),
            pltpu.VMEM((tokens, width), BF16),
            pltpu.VMEM((tokens, width), BF16),
            pltpu.VMEM(tile, BF16),
            pltpu.VMEM(tile, BF16),
            pltpu.VMEM(tile, F32),
            pltpu.VMEM(tile, F32),
            pltpu.VMEM((count, BLOCK), F32),
            pltpu.VMEM((count, LANES), F32),
            pltpu.VMEM(state, F32),
            pltpu.VMEM(message, F32),
        ),
        in_specs=[pl.BlockSpec(memory_space=pltpu.HBM)] * 8,
        out_specs=(vmem,) * 11,
        scratch_shapes=[
            pltpu.VMEM((count, BLOCK), F32),
            pltpu.VMEM((count, BLOCK, LANES), F32),
            pltpu.VMEM((count, BLOCK), F32),
            pltpu.VMEM((blocks, BLOCK, BLOCK), F32),
            pltpu.VMEM((count, BLOCK, BLOCK), F32),
            pltpu.VMEM((count, BLOCK, BLOCK), BF16),
            pltpu.VMEM(tile, BF16),
            pltpu.VMEM((heads, D_HEAD, LANES), F32),
            pltpu.VMEM(tile, F32),
            pltpu.VMEM(tile, F32),
            pltpu.VMEM(tile, F32),
            pltpu.VMEM(tile, F32),
            pltpu.VMEM(state, F32),
            pltpu.VMEM(state, F32),
            pltpu.VMEM(message, F32),
            pltpu.VMEM((2, steps) + message, F32),
            pltpu.VMEM((2, steps) + message, F32),
            pltpu.VMEM((blocks, 8, LANES), F32),
            pltpu.VMEM((blocks, tp_count - 1, 8, LANES), F32),
            pltpu.SMEM(offsets.shape, jnp.int32),
            pltpu.VMEM((tokens, width), BF16),
            pltpu.VMEM((tokens, width), BF16),
            pltpu.VMEM((tokens, width), BF16),
            pltpu.VMEM((tokens, width), BF16),
            pltpu.VMEM((1, width), F32),
            pltpu.VMEM(log_decay.shape, F32),
            pltpu.VMEM((tokens, width), BF16),
            pltpu.SemaphoreType.DMA((2, steps, heads)),
            pltpu.SemaphoreType.DMA((2, steps, heads)),
            pltpu.SemaphoreType.DMA((blocks, tp_count - 1)),
            pltpu.SemaphoreType.DMA((blocks, tp_count - 1)),
            pltpu.SemaphoreType.DMA((8,)),
        ],
        compiler_params=pltpu.CompilerParams(
            collective_id=0, has_side_effects=True, vmem_limit_bytes=44 * 1024 * 1024
        ),
    )(*[
        pltpu.with_memory_space_constraint(array, pltpu.HBM)
        for array in (
            offsets, query_rows, key_rows, value_rows, gate_logits,
            norm_gain.reshape(1, width), log_decay, cotangent,
        )
    ])
    return pl.pallas_call(
        functools.partial(finish_kernel, heads, blocks),
        out_shape=(out,) * 5,
        in_specs=[vmem] * 11,
        out_specs=(anywhere,) * 5,
        scratch_shapes=[
            pltpu.VMEM((tokens, width), BF16),
            pltpu.VMEM((tokens, width), BF16),
            pltpu.VMEM((heads, D_HEAD, LANES), F32),
            pltpu.SemaphoreType.DMA((3,)),
            pltpu.SemaphoreType.DMA((blocks, 2)),
        ],
        compiler_params=pltpu.CompilerParams(vmem_limit_bytes=24 * 1024 * 1024),
    )(*held)


def solution(mesh):
    rows = P("ctx", "tp")
    return jax.shard_map(
        functools.partial(local, mesh.shape["ctx"], mesh.shape["tp"]),
        mesh=mesh,
        in_specs=(rows, rows, rows, rows, P("tp"), P("tp", "ctx"), P(), rows),
        out_specs=(rows,) * 5,
        check_vma=False,
    )
```

```python
import functools

import jax
import jax.numpy as jnp
from jax import lax
from jax.experimental import pallas as pl
from jax.experimental.pallas import tpu as pltpu
from jax.sharding import PartitionSpec as P

D_HEAD = 128
BLOCK = 512
HALF = 256
LANES = 128
EPS_NORM = 1e-06
MASKED = -1000.0
MESH = pl.DeviceIdType.MESH
F32 = jnp.float32
BF16 = jnp.bfloat16


def split(value):
    high = value.astype(BF16)
    return high, (value - high.astype(F32)).astype(BF16)


def dot(left, right, dims):
    return lax.dot_general(left, right, (dims, ((), ())), preferred_element_type=F32)


def mm(left, right):
    return dot(left, right, ((1,), (0,)))


def mm_rt(left, right):
    return dot(left, right, ((1,), (1,)))


def twice(rows):
    return jnp.concatenate([rows, rows], axis=0)


def state_times(state, columns):
    return mm(jnp.concatenate(split(state), axis=1), twice(columns))


def outer_state(columns, weighted):
    both = mm_rt(columns, jnp.concatenate(split(weighted), axis=0))
    return both[:, :D_HEAD] + both[:, D_HEAD:]


def causal(left, right, product):
    first = product(left[:, :HALF], right[0])
    second = product(left[:, HALF:], right[1])
    return jnp.concatenate([first[:, :HALF], first[:, HALF:] + second], axis=1)


def kernel(
    ctx_count, tp_count, heads, blocks,
    offs_hbm, q_hbm, k_hbm, v_hbm, gate_hbm, gain_hbm, decay_hbm, cot_hbm,
    att_ref, dq_ref, dk_ref, dv_ref, dg_ref,
    key_cols, value_cols, key_acc, value_acc, last, factor, back_state, prefix,
    run_row, run_col, carry, bias, within, weights,
    query_cols, gain_cols, attn, sig, upstream, gattn, states, local_state,
    total, send_state, recv_state, sums, recv_sums,
    offs, q_ref, k_ref, v_ref, gate_ref, gain_ref, decay_ref, cot_ref,
    send_sem, recv_sem, sum_send_sem, sum_recv_sem, load_sem,
):
    loads = [
        pltpu.make_async_copy(src, dst, load_sem.at[i])
        for i, (src, dst) in enumerate((
            (decay_hbm, decay_ref), (offs_hbm, offs), (k_hbm, k_ref), (v_hbm, v_ref),
            (q_hbm, q_ref), (gate_hbm, gate_ref), (cot_hbm, cot_ref), (gain_hbm, gain_ref),
        ))
    ]
    for load in loads:
        load.start()
    ctx = lax.axis_index("ctx")
    tp = lax.axis_index("tp")
    steps = (ctx_count - 1).bit_length()
    features = tp_count * heads * D_HEAD
    offset_count = offs.shape[0]

    def partner(step):
        size = 1 << step
        return ctx + size * (1 - 2 * ((ctx // size) % 2))

    def peer(hop):
        return lax.rem(tp + hop, tp_count)

    barrier = pltpu.get_barrier_semaphore()
    for step in range(steps):
        pl.semaphore_signal(barrier, inc=1, device_id=(partner(step), tp), device_id_type=MESH)
    for hop in range(1, tp_count):
        pl.semaphore_signal(barrier, inc=1, device_id=(ctx, peer(hop)), device_id_type=MESH)

    first = ctx * (blocks * BLOCK)

    def segment(positions):
        count = (offs[0] <= positions).astype(jnp.int32)
        for entry in range(1, offset_count):
            count = count + (offs[entry] <= positions).astype(jnp.int32)
        return count

    loads[0].wait()
    loads[1].wait()
    decays = jnp.concatenate(
        [decay_ref[:, b * BLOCK:(b + 1) * BLOCK] for b in range(blocks)], axis=0
    )
    rest = decays
    pieces = []
    for _ in range(3):
        piece = rest.astype(BF16)
        pieces.append(piece)
        rest = rest - piece.astype(F32)
    lower = lax.broadcasted_iota(jnp.int32, (BLOCK, BLOCK), 0)
    upper = lax.broadcasted_iota(jnp.int32, (BLOCK, BLOCK), 1)
    summing = jnp.where(lower <= upper, 1.0, 0.0).astype(BF16)
    running = mm(pieces[2], summing) + mm(pieces[1], summing) + mm(pieces[0], summing)
    run_row[...] = running
    lane = lax.broadcasted_iota(jnp.int32, (1, BLOCK), 1)
    sub = lax.broadcasted_iota(jnp.int32, (BLOCK, 1), 0)
    last_rows = []
    for b in range(blocks):
        start = first + b * BLOCK
        rows = running[b * heads:(b + 1) * heads]
        seg_row = segment(start + lane)
        before = segment(start - 1)
        final = segment(start + BLOCK - 1)
        end = rows[:, BLOCK - 1:]
        last_rows.append(jnp.where(seg_row == final, jnp.exp(jnp.minimum(end - rows, 0.0)), 0.0))
        whole = jnp.where(before == final, jnp.exp(end), 0.0)
        factor[b * heads:(b + 1) * heads, :] = jnp.broadcast_to(whole, (heads, LANES))
    count = heads * blocks
    last[...] = jnp.concatenate(last_rows, axis=0)
    def head_cols(h):
        return pl.ds(pl.multiple_of(h * D_HEAD, D_HEAD), D_HEAD)

    def block_rows(b):
        return pl.ds(b * BLOCK, BLOCK)

    def factor_of(b, h):
        return factor[pl.ds(b * heads + h, 1), :]

    def exchange(way, step, h):
        return pltpu.make_async_remote_copy(
            src_ref=send_state.at[way, step, h],
            dst_ref=recv_state.at[way, step, h],
            send_sem=send_sem.at[way, step, h],
            recv_sem=recv_sem.at[way, step, h],
            device_id=(partner(step), tp),
            device_id_type=MESH,
        )

    def begin(way, h, state, state_factor):
        prefix[h, :D_HEAD, :] = jnp.zeros((D_HEAD, LANES), F32)
        prefix[h, D_HEAD:, :] = jnp.ones((8, LANES), F32)
        spread = jnp.broadcast_to(state_factor, (8, LANES))
        total[h, :D_HEAD, :] = state
        total[h, D_HEAD:, :] = spread
        send_state[way, 0, h, :D_HEAD, :] = state
        send_state[way, 0, h, D_HEAD:, :] = spread
        exchange(way, 0, h).start()

    def advance(way, step, h):
        exchange(way, step, h).wait()
        size = 1 << step
        bit = (ctx // size) % 2
        after = bit == 1 if way == 0 else bit == 0
        other = recv_state[way, step, h, :D_HEAD, :]
        other_factor = recv_state[way, step, h, D_HEAD:, :][:1]
        mine = total[h, :D_HEAD, :]
        my_factor = total[h, D_HEAD:, :][:1]
        if step + 1 < steps:
            joined = jnp.where(after, my_factor * other + mine, other_factor * mine + other)
            spread = jnp.broadcast_to(my_factor * other_factor, (8, LANES))
            send_state[way, step + 1, h, :D_HEAD, :] = joined
            send_state[way, step + 1, h, D_HEAD:, :] = spread
            exchange(way, step + 1, h).start()
            total[h, :D_HEAD, :] = joined
            total[h, D_HEAD:, :] = spread
        so_far = prefix[h, :D_HEAD, :]
        so_far_factor = prefix[h, D_HEAD:, :][:1]
        prefix[h, :D_HEAD, :] = jnp.where(after, so_far_factor * other + so_far, so_far)
        prefix[h, D_HEAD:, :] = jnp.broadcast_to(
            jnp.where(after, so_far_factor * other_factor, so_far_factor), (8, LANES)
        )

    def join_early(way, h):
        if steps > 1:
            @pl.when(h > 0)
            def _():
                advance(way, 0, h - 1)

            @pl.when(h == heads - 1)
            def _():
                advance(way, 0, h)

    def advance_rest(way):
        for step in range(1, steps - 1):
            for h in range(heads):
                advance(way, step, h)

    pl.semaphore_wait(barrier, steps + tp_count - 1)
    loads[2].wait()
    loads[3].wait()

    def summarize(h, _):
        cols = head_cols(h)
        acc = None
        prod = None
        for b in range(blocks):
            r = b * heads + h
            key = k_ref[block_rows(b), cols].T
            value = v_ref[block_rows(b), cols].T
            key_cols[r] = key
            value_cols[r] = value
            state = outer_state(value, key.astype(F32) * last[pl.ds(r, 1), :])
            local_state[r] = state
            fac = factor_of(b, h)
            acc = state if acc is None else fac * acc + state
            prod = fac if prod is None else prod * fac
        begin(0, h, acc, prod)
        return 0

    lax.fori_loop(0, heads, summarize, 0, unroll=True)

    carry_rows = []
    for b in range(blocks):
        start = first + b * BLOCK
        seg_row = segment(start + lane)
        seg_col = segment(start + sub)
        bias[b] = jnp.where((seg_col == seg_row) & (lower <= upper), 0.0, MASKED)
        rows = running[b * heads:(b + 1) * heads]
        carry_rows.append(jnp.where(seg_row == segment(start - 1), jnp.exp(rows), 0.0))
    carry[...] = jnp.concatenate(carry_rows, axis=0)
    columns = jnp.concatenate([running, jnp.zeros((LANES - count, BLOCK), F32)], axis=0).T
    for r in range(count):
        run_col[r] = jnp.broadcast_to(columns[:, r:r + 1], (BLOCK, LANES))

    for load in loads[4:]:
        load.wait()
    def attend(h, _):
        cols = head_cols(h)
        join_early(0, h)
        gain = jnp.broadcast_to(gain_ref[:, cols], (D_HEAD, LANES)).T
        gain_cols[h] = gain
        gain = jnp.concatenate([gain] * (BLOCK // LANES), axis=1)
        for b in range(blocks):
            r = b * heads + h
            rows = block_rows(b)
            query = q_ref[rows, cols].T
            query_cols[r] = query
            parts = []
            for top in (0, HALF):
                half = slice(top, top + HALF)
                col = run_col[r, half, :]
                col = jnp.concatenate([col] * ((BLOCK - top) // LANES), axis=1)
                row = run_row[pl.ds(r, 1), :][:, top:]
                decay = jnp.exp(jnp.minimum(row - col, bias[b, half, top:]))
                within[r, half, top:] = decay
                scores = mm(k_ref[pl.ds(b * BLOCK + top, HALF), cols], query[:, top:])
                weight = (scores * decay).astype(BF16)
                weights[r, half, top:] = weight
                parts.append(weight)
            attn[r] = causal(value_cols[r], parts, mm)
            gate = jax.nn.sigmoid(gate_ref[rows, cols].T.astype(F32))
            sig[r] = gate
            upstream[r] = cot_ref[rows, cols].T.astype(F32) * (gain * gate)
        return 0

    lax.fori_loop(0, heads, attend, 0, unroll=True)
    advance_rest(0)

    def sum_copy(hop):
        return pltpu.make_async_remote_copy(
            src_ref=sums,
            dst_ref=recv_sums.at[hop - 1],
            send_sem=sum_send_sem.at[hop - 1],
            recv_sem=sum_recv_sem.at[hop - 1],
            device_id=(ctx, peer(hop)),
            device_id_type=MESH,
        )

    chunks = BLOCK // LANES

    def carry_in(h, acc):
        if steps > 0:
            advance(0, steps - 1, h)
        state = prefix[h, :D_HEAD, :]
        added = []
        for b in range(blocks):
            r = b * heads + h
            states[r] = state
            value = attn[r] + carry[pl.ds(r, 1), :] * state_times(state, query_cols[r])
            attn[r] = value
            if b + 1 < blocks:
                state = factor_of(b, h) * state + local_state[r]
            added.append(acc[2 * b] + jnp.sum(value * value, axis=0, keepdims=True))
            added.append(acc[2 * b + 1] + jnp.sum(upstream[r] * value, axis=0, keepdims=True))
        return tuple(added)

    zero = jnp.zeros((1, BLOCK), F32)
    lines = lax.fori_loop(0, heads, carry_in, (zero,) * (2 * blocks), unroll=True)
    for at, line in enumerate(lines):
        for c in range(chunks):
            sums[at, c:c + 1, :] = line[:, c * LANES:(c + 1) * LANES]
    for hop in range(1, tp_count):
        sum_copy(hop).start()
    added = sums[...]
    for hop in range(1, tp_count):
        sum_copy(hop).wait()
        added = added + recv_sums[hop - 1]
    scales, inner_scales = [], []
    for b in range(blocks):
        inverse = 1.0 / jnp.sqrt(added[2 * b] / features + EPS_NORM)
        mean_inner = added[2 * b + 1] * inverse / features
        inv, mean_inner = (
            jnp.concatenate([part[c:c + 1] for c in range(chunks)], axis=1)
            for part in (inverse, mean_inner)
        )
        scales.append(inv)
        inner_scales.append(inv * mean_inner)

    def grad_in(h, _):
        acc = None
        prod = None
        for b in range(blocks - 1, -1, -1):
            r = b * heads + h
            grad = (upstream[r] - attn[r] * inner_scales[b]) * scales[b]
            gattn[r] = grad
            state = outer_state(query_cols[r], grad * carry[pl.ds(r, 1), :])
            back_state[r] = state
            fac = factor_of(b, h)
            acc = state if acc is None else fac * acc + state
            prod = fac if prod is None else prod * fac
        begin(1, h, acc, prod)
        return 0

    lax.fori_loop(0, heads, grad_in, 0, unroll=True)

    def retreat(h, _):
        cols = head_cols(h)
        join_early(1, h)
        gain = jnp.concatenate([gain_cols[h]] * (BLOCK // LANES), axis=1)
        for b in range(blocks):
            r = b * heads + h
            rows = block_rows(b)
            high, low = split(gattn[r])
            parts = []
            for top in (0, HALF):
                half = slice(top, top + HALF)
                scores = mm(v_ref[pl.ds(b * BLOCK + top, HALF), cols], high[:, top:])
                parts.append((scores * within[r, half, top:]).astype(BF16))
            state_high, state_low = split(states[r].T)
            crossed = mm(
                jnp.concatenate([state_high, state_high], axis=1),
                jnp.concatenate([high, low], axis=0),
            ) + mm(state_low, high)
            dq = causal(key_cols[r], parts, mm) + carry[pl.ds(r, 1), :] * crossed
            dq_ref[rows, cols] = dq.astype(BF16).T
            query = query_cols[r]
            key_acc[r, :, :HALF] = mm_rt(query, parts[0])
            key_acc[r, :, HALF:] = mm_rt(query[:, HALF:], parts[1])
            value_acc[r, :, :HALF] = mm_rt(high, weights[r, :HALF, :])
            value_acc[r, :, HALF:] = mm_rt(high[:, HALF:], weights[r, HALF:, HALF:])
            normed = attn[r] * scales[b]
            gate = sig[r]
            att_ref[rows, cols] = (normed * (gain * gate)).astype(BF16).T
            dg_ref[rows, cols] = (upstream[r] * normed * (1.0 - gate)).astype(BF16).T
        return 0

    lax.fori_loop(0, heads, retreat, 0, unroll=True)
    advance_rest(1)

    def finish(h, _):
        cols = head_cols(h)
        if steps > 0:
            advance(1, steps - 1, h)
        coming = prefix[h, :D_HEAD, :]
        for b in range(blocks - 1, -1, -1):
            r = b * heads + h
            rows = block_rows(b)
            weight = last[pl.ds(r, 1), :]
            dk = key_acc[r] + weight * state_times(coming, value_cols[r])
            dv = value_acc[r] + weight * state_times(coming.T, key_cols[r])
            dk_ref[rows, cols] = dk.astype(BF16).T
            dv_ref[rows, cols] = dv.astype(BF16).T
            if b > 0:
                coming = factor_of(b, h) * coming + back_state[r]
        return 0

    lax.fori_loop(0, heads, finish, 0, unroll=True)


def write_kernel(count, *refs):
    copies = [
        pltpu.make_async_copy(refs[i], refs[count + i], refs[2 * count].at[i]) for i in range(count)
    ]
    for copy in copies:
        copy.start()
    for copy in copies:
        copy.wait()


def local(ctx_count, tp_count, query_rows, key_rows, value_rows, gate_logits, norm_gain, log_decay,
          offsets, cotangent):
    heads = log_decay.shape[0]
    tokens, width = query_rows.shape
    blocks = tokens // BLOCK
    count = heads * blocks
    steps = (ctx_count - 1).bit_length()
    out = jax.ShapeDtypeStruct((tokens, width), BF16)
    vmem = pl.BlockSpec(memory_space=pltpu.VMEM)
    anywhere = pl.BlockSpec(memory_space=pl.ANY)
    tile = (count, D_HEAD, BLOCK)
    state = (count, D_HEAD, D_HEAD)
    message = (heads, D_HEAD + 8, LANES)
    held = pl.pallas_call(
        functools.partial(kernel, ctx_count, tp_count, heads, blocks),
        out_shape=(pltpu.VMEM((tokens, width), BF16),) * 5,
        in_specs=[pl.BlockSpec(memory_space=pltpu.HBM)] * 8,
        out_specs=(vmem,) * 5,
        scratch_shapes=[
            pltpu.VMEM(tile, BF16),
            pltpu.VMEM(tile, BF16),
            pltpu.VMEM(tile, F32),
            pltpu.VMEM(tile, F32),
            pltpu.VMEM((count, BLOCK), F32),
            pltpu.VMEM((count, LANES), F32),
            pltpu.VMEM(state, F32),
            pltpu.VMEM(message, F32),
            pltpu.VMEM((count, BLOCK), F32),
            pltpu.VMEM((count, BLOCK, LANES), F32),
            pltpu.VMEM((count, BLOCK), F32),
            pltpu.VMEM((blocks, BLOCK, BLOCK), F32),
            pltpu.VMEM((count, BLOCK, BLOCK), F32),
            pltpu.VMEM((count, BLOCK, BLOCK), BF16),
            pltpu.VMEM(tile, BF16),
            pltpu.VMEM((heads, D_HEAD, LANES), F32),
            pltpu.VMEM(tile, F32),
            pltpu.VMEM(tile, F32),
            pltpu.VMEM(tile, F32),
            pltpu.VMEM(tile, F32),
            pltpu.VMEM(state, F32),
            pltpu.VMEM(state, F32),
            pltpu.VMEM(message, F32),
            pltpu.VMEM((2, steps) + message, F32),
            pltpu.VMEM((2, steps) + message, F32),
            pltpu.VMEM((2 * blocks, BLOCK // LANES, LANES), F32),
            pltpu.VMEM((tp_count - 1, 2 * blocks, BLOCK // LANES, LANES), F32),
            pltpu.SMEM(offsets.shape, jnp.int32),
            pltpu.VMEM((tokens, width), BF16),
            pltpu.VMEM((tokens, width), BF16),
            pltpu.VMEM((tokens, width), BF16),
            pltpu.VMEM((tokens, width), BF16),
            pltpu.VMEM((1, width), F32),
            pltpu.VMEM(log_decay.shape, F32),
            pltpu.VMEM((tokens, width), BF16),
            pltpu.SemaphoreType.DMA((2, steps, heads)),
            pltpu.SemaphoreType.DMA((2, steps, heads)),
            pltpu.SemaphoreType.DMA((tp_count - 1,)),
            pltpu.SemaphoreType.DMA((tp_count - 1,)),
            pltpu.SemaphoreType.DMA((8,)),
        ],
        compiler_params=pltpu.CompilerParams(
            collective_id=0, has_side_effects=True, vmem_limit_bytes=52 * 1024 * 1024
        ),
    )(*[
        pltpu.with_memory_space_constraint(array, pltpu.HBM)
        for array in (
            offsets, query_rows, key_rows, value_rows, gate_logits,
            norm_gain.reshape(1, width), log_decay, cotangent,
        )
    ])
    return pl.pallas_call(
        functools.partial(write_kernel, 5),
        out_shape=(out,) * 5,
        in_specs=[vmem] * 5,
        out_specs=(anywhere,) * 5,
        scratch_shapes=[pltpu.SemaphoreType.DMA((5,))],
    )(*held)


def solution(mesh):
    rows = P("ctx", "tp")
    return jax.shard_map(
        functools.partial(local, mesh.shape["ctx"], mesh.shape["tp"]),
        mesh=mesh,
        in_specs=(rows, rows, rows, rows, P("tp"), P("tp", "ctx"), P(), rows),
        out_specs=(rows,) * 5,
        check_vma=False,
    )
```

```python
import functools

import jax
import jax.numpy as jnp
from jax import lax
from jax.experimental import pallas as pl
from jax.experimental.pallas import tpu as pltpu
from jax.sharding import PartitionSpec as P

D_HEAD = 128
BLOCK = 512
HALF = 256
LANES = 128
EPS_NORM = 1e-06
MASKED = -1000.0
MESH = pl.DeviceIdType.MESH
F32 = jnp.float32
BF16 = jnp.bfloat16


def split(value):
    high = value.astype(BF16)
    return high, (value - high.astype(F32)).astype(BF16)


def dot(left, right, dims):
    return lax.dot_general(left, right, (dims, ((), ())), preferred_element_type=F32)


def mm(left, right):
    return dot(left, right, ((1,), (0,)))


def mm_rt(left, right):
    return dot(left, right, ((1,), (1,)))


def twice(rows):
    return jnp.concatenate([rows, rows], axis=0)


def state_times(state, columns):
    return mm(jnp.concatenate(split(state), axis=1), twice(columns))


def outer_state(columns, weighted):
    both = mm_rt(columns, jnp.concatenate(split(weighted), axis=0))
    return both[:, :D_HEAD] + both[:, D_HEAD:]


def causal(left, right, product):
    first = product(left[:, :HALF], right[0])
    second = product(left[:, HALF:], right[1])
    return jnp.concatenate([first[:, :HALF], first[:, HALF:] + second], axis=1)


def kernel(
    ctx_count, tp_count, heads, blocks,
    offs_hbm, q_hbm, k_hbm, v_hbm, gate_hbm, gain_hbm, decay_hbm, cot_hbm,
    att_ref, dq_ref, dk_ref, dv_ref, dg_ref,
    key_cols, value_cols, key_acc, value_acc, last, factor, back_state, prefix,
    run_row, run_col, carry, bias, within, weights,
    query_cols, gain_cols, attn, sig, upstream, gattn, states, local_state,
    total, send_state, recv_state, sums, recv_sums,
    offs, q_ref, k_ref, v_ref, gate_ref, gain_ref, decay_ref, cot_ref,
    send_sem, recv_sem, sum_send_sem, sum_recv_sem, load_sem,
):
    loads = [
        pltpu.make_async_copy(src, dst, load_sem.at[i])
        for i, (src, dst) in enumerate((
            (decay_hbm, decay_ref), (offs_hbm, offs), (k_hbm, k_ref), (v_hbm, v_ref),
            (q_hbm, q_ref), (gate_hbm, gate_ref), (cot_hbm, cot_ref), (gain_hbm, gain_ref),
        ))
    ]
    for load in loads:
        load.start()
    ctx = lax.axis_index("ctx")
    tp = lax.axis_index("tp")
    steps = (ctx_count - 1).bit_length()
    features = tp_count * heads * D_HEAD
    offset_count = offs.shape[0]

    def partner(step):
        size = 1 << step
        return ctx + size * (1 - 2 * ((ctx // size) % 2))

    def peer(hop):
        return lax.rem(tp + hop, tp_count)

    barrier = pltpu.get_barrier_semaphore()
    for step in range(steps):
        pl.semaphore_signal(barrier, inc=1, device_id=(partner(step), tp), device_id_type=MESH)
    for hop in range(1, tp_count):
        pl.semaphore_signal(barrier, inc=1, device_id=(ctx, peer(hop)), device_id_type=MESH)

    first = ctx * (blocks * BLOCK)

    def segment(positions):
        count = (offs[0] <= positions).astype(jnp.int32)
        for entry in range(1, offset_count):
            count = count + (offs[entry] <= positions).astype(jnp.int32)
        return count

    loads[0].wait()
    loads[1].wait()
    decays = jnp.concatenate(
        [decay_ref[:, b * BLOCK:(b + 1) * BLOCK] for b in range(blocks)], axis=0
    )
    rest = decays
    pieces = []
    for _ in range(3):
        piece = rest.astype(BF16)
        pieces.append(piece)
        rest = rest - piece.astype(F32)
    lower = lax.broadcasted_iota(jnp.int32, (BLOCK, BLOCK), 0)
    upper = lax.broadcasted_iota(jnp.int32, (BLOCK, BLOCK), 1)
    summing = jnp.where(lower <= upper, 1.0, 0.0).astype(BF16)
    running = mm(pieces[2], summing) + mm(pieces[1], summing) + mm(pieces[0], summing)
    run_row[...] = running
    lane = lax.broadcasted_iota(jnp.int32, (1, BLOCK), 1)
    sub = lax.broadcasted_iota(jnp.int32, (BLOCK, 1), 0)
    last_rows = []
    for b in range(blocks):
        start = first + b * BLOCK
        rows = running[b * heads:(b + 1) * heads]
        seg_row = segment(start + lane)
        before = segment(start - 1)
        final = segment(start + BLOCK - 1)
        end = rows[:, BLOCK - 1:]
        last_rows.append(jnp.where(seg_row == final, jnp.exp(jnp.minimum(end - rows, 0.0)), 0.0))
        whole = jnp.where(before == final, jnp.exp(end), 0.0)
        factor[b * heads:(b + 1) * heads, :] = jnp.broadcast_to(whole, (heads, LANES))
    count = heads * blocks
    last[...] = jnp.concatenate(last_rows, axis=0)
    def head_cols(h):
        return pl.ds(pl.multiple_of(h * D_HEAD, D_HEAD), D_HEAD)

    def block_rows(b):
        return pl.ds(b * BLOCK, BLOCK)

    def factor_of(b, h):
        return factor[pl.ds(b * heads + h, 1), :]

    def exchange(way, step, h):
        return pltpu.make_async_remote_copy(
            src_ref=send_state.at[way, step, h],
            dst_ref=recv_state.at[way, step, h],
            send_sem=send_sem.at[way, step, h],
            recv_sem=recv_sem.at[way, step, h],
            device_id=(partner(step), tp),
            device_id_type=MESH,
        )

    def begin(way, h, state, state_factor):
        prefix[h, :D_HEAD, :] = jnp.zeros((D_HEAD, LANES), F32)
        prefix[h, D_HEAD:, :] = jnp.ones((8, LANES), F32)
        spread = jnp.broadcast_to(state_factor, (8, LANES))
        total[h, :D_HEAD, :] = state
        total[h, D_HEAD:, :] = spread
        send_state[way, 0, h, :D_HEAD, :] = state
        send_state[way, 0, h, D_HEAD:, :] = spread
        exchange(way, 0, h).start()

    def advance(way, step, h):
        exchange(way, step, h).wait()
        size = 1 << step
        bit = (ctx // size) % 2
        after = bit == 1 if way == 0 else bit == 0
        other = recv_state[way, step, h, :D_HEAD, :]
        other_factor = recv_state[way, step, h, D_HEAD:, :][:1]
        mine = total[h, :D_HEAD, :]
        my_factor = total[h, D_HEAD:, :][:1]
        if step + 1 < steps:
            joined = jnp.where(after, my_factor * other + mine, other_factor * mine + other)
            spread = jnp.broadcast_to(my_factor * other_factor, (8, LANES))
            send_state[way, step + 1, h, :D_HEAD, :] = joined
            send_state[way, step + 1, h, D_HEAD:, :] = spread
            exchange(way, step + 1, h).start()
            total[h, :D_HEAD, :] = joined
            total[h, D_HEAD:, :] = spread
        so_far = prefix[h, :D_HEAD, :]
        so_far_factor = prefix[h, D_HEAD:, :][:1]
        prefix[h, :D_HEAD, :] = jnp.where(after, so_far_factor * other + so_far, so_far)
        prefix[h, D_HEAD:, :] = jnp.broadcast_to(
            jnp.where(after, so_far_factor * other_factor, so_far_factor), (8, LANES)
        )

    def join_early(way, h):
        if steps > 1:
            @pl.when(h > 0)
            def _():
                advance(way, 0, h - 1)

            @pl.when(h == heads - 1)
            def _():
                advance(way, 0, h)

    def advance_rest(way):
        for step in range(1, steps - 1):
            for h in range(heads):
                advance(way, step, h)

    pl.semaphore_wait(barrier, steps + tp_count - 1)
    loads[2].wait()
    loads[3].wait()

    def summarize(h, _):
        cols = head_cols(h)
        acc = None
        prod = None
        for b in range(blocks):
            r = b * heads + h
            key = k_ref[block_rows(b), cols].T
            value = v_ref[block_rows(b), cols].T
            key_cols[r] = key
            value_cols[r] = value
            state = outer_state(value, key.astype(F32) * last[pl.ds(r, 1), :])
            local_state[r] = state
            fac = factor_of(b, h)
            acc = state if acc is None else fac * acc + state
            prod = fac if prod is None else prod * fac
        begin(0, h, acc, prod)
        return 0

    lax.fori_loop(0, heads, summarize, 0, unroll=True)

    carry_rows = []
    for b in range(blocks):
        start = first + b * BLOCK
        seg_row = segment(start + lane)
        seg_col = segment(start + sub)
        bias[b] = jnp.where((seg_col == seg_row) & (lower <= upper), 0.0, MASKED)
        rows = running[b * heads:(b + 1) * heads]
        carry_rows.append(jnp.where(seg_row == segment(start - 1), jnp.exp(rows), 0.0))
    carry[...] = jnp.concatenate(carry_rows, axis=0)
    columns = jnp.concatenate([running, jnp.zeros((LANES - count, BLOCK), F32)], axis=0).T
    for r in range(count):
        run_col[r] = jnp.broadcast_to(columns[:, r:r + 1], (BLOCK, LANES))

    for load in loads[4:]:
        load.wait()
    def attend(h, _):
        cols = head_cols(h)
        join_early(0, h)
        gain = jnp.broadcast_to(gain_ref[:, cols], (D_HEAD, LANES)).T
        gain_cols[h] = gain
        gain = jnp.concatenate([gain] * (BLOCK // LANES), axis=1)
        for b in range(blocks):
            r = b * heads + h
            rows = block_rows(b)
            query = q_ref[rows, cols].T
            query_cols[r] = query
            parts = []
            for top in (0, HALF):
                half = slice(top, top + HALF)
                col = run_col[r, half, :]
                col = jnp.concatenate([col] * ((BLOCK - top) // LANES), axis=1)
                row = run_row[pl.ds(r, 1), :][:, top:]
                decay = jnp.exp(jnp.minimum(row - col, bias[b, half, top:]))
                within[r, half, top:] = decay
                scores = mm(k_ref[pl.ds(b * BLOCK + top, HALF), cols], query[:, top:])
                weight = (scores * decay).astype(BF16)
                weights[r, half, top:] = weight
                parts.append(weight)
            attn[r] = causal(value_cols[r], parts, mm)
            gate = jax.nn.sigmoid(gate_ref[rows, cols].T.astype(F32))
            sig[r] = gate
            upstream[r] = cot_ref[rows, cols].T.astype(F32) * (gain * gate)
        return 0

    lax.fori_loop(0, heads, attend, 0, unroll=True)
    advance_rest(0)

    def sum_copy(hop):
        return pltpu.make_async_remote_copy(
            src_ref=sums,
            dst_ref=recv_sums.at[hop - 1],
            send_sem=sum_send_sem.at[hop - 1],
            recv_sem=sum_recv_sem.at[hop - 1],
            device_id=(ctx, peer(hop)),
            device_id_type=MESH,
        )

    chunks = BLOCK // LANES

    def carry_in(h, acc):
        if steps > 0:
            advance(0, steps - 1, h)
        state = prefix[h, :D_HEAD, :]
        added = []
        for b in range(blocks):
            r = b * heads + h
            states[r] = state
            value = attn[r] + carry[pl.ds(r, 1), :] * state_times(state, query_cols[r])
            attn[r] = value
            if b + 1 < blocks:
                state = factor_of(b, h) * state + local_state[r]
            added.append(acc[2 * b] + jnp.sum(value * value, axis=0, keepdims=True))
            added.append(acc[2 * b + 1] + jnp.sum(upstream[r] * value, axis=0, keepdims=True))
        return tuple(added)

    zero = jnp.zeros((1, BLOCK), F32)
    lines = lax.fori_loop(0, heads, carry_in, (zero,) * (2 * blocks), unroll=True)
    for at, line in enumerate(lines):
        for c in range(chunks):
            sums[at, c:c + 1, :] = line[:, c * LANES:(c + 1) * LANES]
    for hop in range(1, tp_count):
        sum_copy(hop).start()
    added = sums[...]
    for hop in range(1, tp_count):
        sum_copy(hop).wait()
        added = added + recv_sums[hop - 1]
    scales, inner_scales = [], []
    for b in range(blocks):
        inverse = 1.0 / jnp.sqrt(added[2 * b] / features + EPS_NORM)
        mean_inner = added[2 * b + 1] * inverse / features
        inv, mean_inner = (
            jnp.concatenate([part[c:c + 1] for c in range(chunks)], axis=1)
            for part in (inverse, mean_inner)
        )
        scales.append(inv)
        inner_scales.append(inv * mean_inner)

    def grad_in(h, _):
        acc = None
        prod = None
        for b in range(blocks - 1, -1, -1):
            r = b * heads + h
            grad = (upstream[r] - attn[r] * inner_scales[b]) * scales[b]
            gattn[r] = grad
            state = outer_state(query_cols[r], grad * carry[pl.ds(r, 1), :])
            back_state[r] = state
            fac = factor_of(b, h)
            acc = state if acc is None else fac * acc + state
            prod = fac if prod is None else prod * fac
        begin(1, h, acc, prod)
        return 0

    lax.fori_loop(0, heads, grad_in, 0, unroll=True)

    def retreat(h, _):
        cols = head_cols(h)
        join_early(1, h)
        gain = jnp.concatenate([gain_cols[h]] * (BLOCK // LANES), axis=1)
        for b in range(blocks):
            r = b * heads + h
            rows = block_rows(b)
            high, low = split(gattn[r])
            parts = []
            for top in (0, HALF):
                half = slice(top, top + HALF)
                scores = mm(v_ref[pl.ds(b * BLOCK + top, HALF), cols], high[:, top:])
                parts.append((scores * within[r, half, top:]).astype(BF16))
            state_high, state_low = split(states[r].T)
            crossed = mm(
                jnp.concatenate([state_high, state_high], axis=1),
                jnp.concatenate([high, low], axis=0),
            ) + mm(state_low, high)
            dq = causal(key_cols[r], parts, mm) + carry[pl.ds(r, 1), :] * crossed
            dq_ref[rows, cols] = dq.astype(BF16).T
            query = query_cols[r]
            key_acc[r, :, :HALF] = mm_rt(query, parts[0])
            key_acc[r, :, HALF:] = mm_rt(query[:, HALF:], parts[1])
            value_acc[r, :, :HALF] = mm_rt(high, weights[r, :HALF, :])
            value_acc[r, :, HALF:] = mm_rt(high[:, HALF:], weights[r, HALF:, HALF:])
            normed = attn[r] * scales[b]
            gate = sig[r]
            att_ref[rows, cols] = (normed * (gain * gate)).astype(BF16).T
            dg_ref[rows, cols] = (upstream[r] * normed * (1.0 - gate)).astype(BF16).T
        return 0

    lax.fori_loop(0, heads, retreat, 0, unroll=True)
    advance_rest(1)

    def finish(h, _):
        cols = head_cols(h)
        if steps > 0:
            advance(1, steps - 1, h)
        coming = prefix[h, :D_HEAD, :]
        for b in range(blocks - 1, -1, -1):
            r = b * heads + h
            rows = block_rows(b)
            weight = last[pl.ds(r, 1), :]
            dk = key_acc[r] + weight * state_times(coming, value_cols[r])
            dv = value_acc[r] + weight * state_times(coming.T, key_cols[r])
            dk_ref[rows, cols] = dk.astype(BF16).T
            dv_ref[rows, cols] = dv.astype(BF16).T
            if b > 0:
                coming = factor_of(b, h) * coming + back_state[r]
        return 0

    lax.fori_loop(0, heads, finish, 0, unroll=True)


def write_kernel(count, *refs):
    copies = [
        pltpu.make_async_copy(refs[i], refs[count + i], refs[2 * count].at[i]) for i in range(count)
    ]
    for copy in copies:
        copy.start()
    for copy in copies:
        copy.wait()


def local(ctx_count, tp_count, query_rows, key_rows, value_rows, gate_logits, norm_gain, log_decay,
          offsets, cotangent):
    heads = log_decay.shape[0]
    tokens, width = query_rows.shape
    blocks = tokens // BLOCK
    count = heads * blocks
    steps = (ctx_count - 1).bit_length()
    out = jax.ShapeDtypeStruct((tokens, width), BF16)
    vmem = pl.BlockSpec(memory_space=pltpu.VMEM)
    anywhere = pl.BlockSpec(memory_space=pl.ANY)
    tile = (count, D_HEAD, BLOCK)
    state = (count, D_HEAD, D_HEAD)
    message = (heads, D_HEAD + 8, LANES)
    held = pl.pallas_call(
        functools.partial(kernel, ctx_count, tp_count, heads, blocks),
        out_shape=(pltpu.VMEM((tokens, width), BF16),) * 5,
        in_specs=[pl.BlockSpec(memory_space=pltpu.HBM)] * 8,
        out_specs=(vmem,) * 5,
        scratch_shapes=[
            pltpu.VMEM(tile, BF16),
            pltpu.VMEM(tile, BF16),
            pltpu.VMEM(tile, F32),
            pltpu.VMEM(tile, F32),
            pltpu.VMEM((count, BLOCK), F32),
            pltpu.VMEM((count, LANES), F32),
            pltpu.VMEM(state, F32),
            pltpu.VMEM(message, F32),
            pltpu.VMEM((count, BLOCK), F32),
            pltpu.VMEM((count, BLOCK, LANES), F32),
            pltpu.VMEM((count, BLOCK), F32),
            pltpu.VMEM((blocks, BLOCK, BLOCK), F32),
            pltpu.VMEM((count, BLOCK, BLOCK), F32),
            pltpu.VMEM((count, BLOCK, BLOCK), BF16),
            pltpu.VMEM(tile, BF16),
            pltpu.VMEM((heads, D_HEAD, LANES), F32),
            pltpu.VMEM(tile, F32),
            pltpu.VMEM(tile, F32),
            pltpu.VMEM(tile, F32),
            pltpu.VMEM(tile, F32),
            pltpu.VMEM(state, F32),
            pltpu.VMEM(state, F32),
            pltpu.VMEM(message, F32),
            pltpu.VMEM((2, steps) + message, F32),
            pltpu.VMEM((2, steps) + message, F32),
            pltpu.VMEM((2 * blocks, BLOCK // LANES, LANES), F32),
            pltpu.VMEM((tp_count - 1, 2 * blocks, BLOCK // LANES, LANES), F32),
            pltpu.SMEM(offsets.shape, jnp.int32),
            pltpu.VMEM((tokens, width), BF16),
            pltpu.VMEM((tokens, width), BF16),
            pltpu.VMEM((tokens, width), BF16),
            pltpu.VMEM((tokens, width), BF16),
            pltpu.VMEM((1, width), F32),
            pltpu.VMEM(log_decay.shape, F32),
            pltpu.VMEM((tokens, width), BF16),
            pltpu.SemaphoreType.DMA((2, steps, heads)),
            pltpu.SemaphoreType.DMA((2, steps, heads)),
            pltpu.SemaphoreType.DMA((tp_count - 1,)),
            pltpu.SemaphoreType.DMA((tp_count - 1,)),
            pltpu.SemaphoreType.DMA((8,)),
        ],
        compiler_params=pltpu.CompilerParams(
            collective_id=0, has_side_effects=True, vmem_limit_bytes=52 * 1024 * 1024
        ),
    )(*[
        pltpu.with_memory_space_constraint(array, pltpu.HBM)
        for array in (
            offsets, query_rows, key_rows, value_rows, gate_logits,
            norm_gain.reshape(1, width), log_decay, cotangent,
        )
    ])
    return pl.pallas_call(
        functools.partial(write_kernel, 5),
        out_shape=(out,) * 5,
        in_specs=[vmem] * 5,
        out_specs=(anywhere,) * 5,
        scratch_shapes=[pltpu.SemaphoreType.DMA((5,))],
        compiler_params=pltpu.CompilerParams(vmem_limit_bytes=4 * 1024 * 1024),
    )(*held)


def solution(mesh):
    rows = P("ctx", "tp")
    return jax.shard_map(
        functools.partial(local, mesh.shape["ctx"], mesh.shape["tp"]),
        mesh=mesh,
        in_specs=(rows, rows, rows, rows, P("tp"), P("tp", "ctx"), P(), rows),
        out_specs=(rows,) * 5,
        check_vma=False,
    )
```
